1024 devices in a mesh: gx: 16 (over z), gy: 64 (over y, x, core).
Axes of the slice: x: 4, y: 8, z: 16, core: 2. Of those that a mesh axis runs over, the one named last changes fastest.
Arguments:
- displacement: float32 [3, 48, 1536, 384], P(None, 'gx', 'gy'), may hold values from -6 to 6
- applied_load: float32 [3, 48, 1536, 384], P(None, 'gx', 'gy'), may hold values from -6 to 6
- modulus: float32 [48, 1536, 384], P('gx', 'gy'), may hold values from 0.3 to 3
- free_mask: int32 [48, 1536, 384], P('gx', 'gy'), may hold values 0 or 1
- aggregate_shift: int32 [48, 1536, 384], P('gx', 'gy'), may hold values from 0 to 8, as said below
- stencil_table: float32 [27, 3, 3], replicated, as said below
- coarse_inverse: float32 [6, 6, 16, 512, 128], P(None, None, 'gx', 'gy')
Outputs:
- coarse_update: float32 [6, 16, 512, 128], P(None, 'gx', 'gy')
The draws below stay inside these ranges and needn't reach their ends.
Inputs may be any that keep to these rules, and one draw needn't show every extreme that they name: `aggregate_shift`: with sx = code // 3 - 1 and sy = code % 3 - 1: sx is -1 only for nodes in the first plane of their 3x3x3 block along the first dimension and +1 only in its last plane, likewise sy along the second; no node is assigned to an aggregate outside the grid. stencil_table[13] has positive diagonal entries.
All inputs are finite; a program needn't handle non-finite values. No bound on the sum of `free_mask` on one device may be relied on, other than what follows from the above.
Results may differ from the reference program's by a relative error of at most 0.0003.
Values sent between devices are 32-bit elements; how exact they have to be, the bound alone decides.
No kernel may reach another device: no remote copies, remote signals or barrier semaphores. Data moves between devices by JAX's collectives and lax.ppermute only.
A program may use at most 64 MiB of HBM per device.

```python
import math
import jax
import jax.numpy as jnp
from jax import lax

NODES_X = 3
NODES_Y = 24
NODES_Z = 384
GRID_X = 48
GRID_Y = 1536
COARSE_X = 16
COARSE_Y = 512
COARSE_Z = 128


def draw_aggregate_shift(key, part):
    key = jax.random.fold_in(key, 7)
    key_xdir, key_ydir = jax.random.split(key, 2)
    plane_x = jnp.arange(GRID_X, dtype=jnp.int32)[:, None, None]
    plane_y = jnp.arange(GRID_Y, dtype=jnp.int32)[None, :, None]
    percent = 20 + 15 * ((plane_x // NODES_X * 5 + plane_y // NODES_Y * 3) % 4)
    layout = (GRID_X, GRID_Y, NODES_Z)
    roll_x = jax.random.randint(key_xdir, layout, 0, 100, dtype=jnp.int32)
    roll_y = jax.random.randint(key_ydir, layout, 0, 100, dtype=jnp.int32)
    step_x = jnp.where((plane_x % 3 == 0) & (plane_x > 0) & (roll_x < percent), -1, jnp.where((plane_x % 3 == 2) & (plane_x < GRID_X - 1) & (roll_x < percent), 1, 0))
    step_y = jnp.where((plane_y % 3 == 0) & (plane_y > 0) & (roll_y < percent), -1, jnp.where((plane_y % 3 == 2) & (plane_y < GRID_Y - 1) & (roll_y < percent), 1, 0))
    return ((step_x + 1) * 3 + (step_y + 1)).astype(jnp.int32)


def draw_stencil_table(key, part):
    key = jax.random.fold_in(key, 5)
    key_noise, key_lead = jax.random.split(key, 2)
    noise = 0.15 * jax.random.normal(key_noise, (27, 3, 3), jnp.float32)
    lead = jax.random.uniform(key_lead, (3,), jnp.float32, 2.0, 3.0)
    centre = (jnp.arange(27) == 13).astype(jnp.float32)[:, None, None]
    return (noise + centre * jnp.diag(lead)[None]).astype(jnp.float32)


def draw_coarse_inverse(key, part):
    key = jax.random.fold_in(key, 11)
    key_noise, key_lead = jax.random.split(key, 2)
    layout = (6, 6, COARSE_X, COARSE_Y, COARSE_Z)
    noise = 0.3 * jax.random.normal(key_noise, layout, jnp.float32)
    lead = jax.random.uniform(key_lead, layout, jnp.float32, 1.0, 2.0)
    identity = jnp.eye(6, dtype=jnp.float32)[:, :, None, None, None]
    return (0.03 * (identity * lead + (1.0 - identity) * noise)).astype(jnp.float32)


def with_ends(result, own_key, low, high):
    longest = result.shape.index(max(result.shape))
    spots = []
    for shift in (0, 1):
        where = [jax.random.randint(jax.random.fold_in(own_key, axis), (), 0, length) for axis, length in enumerate(result.shape)]
        where[longest] = (where[longest] + shift) % result.shape[longest]
        spots.append(tuple(where))
    return result.at[spots[0]].set(low).at[spots[1]].set(high)


def steps_of(rng, shape, shards, smallest, high):
    def one(position, shards_of):
        heights = jax.random.uniform(jax.random.fold_in(jax.random.fold_in(rng, 6), position), (shards_of,), jnp.float32, smallest / len(shards), high / len(shards))
        return jnp.repeat(jnp.exp(heights), shape[position] // shards_of).reshape((-1,) + (1,) * (len(shape) - position - 1))

    factor_of = one(*shards[0])
    for cut in shards[1:]:
        factor_of = factor_of * one(*cut)
    return factor_of


def scatter_about(stream_key, shape, scale, reach, cuts=(), held_as=jnp.bfloat16):
    result = jax.random.normal(stream_key, shape, jnp.float32) * scale
    if len(cuts) > 0:
        result = steps_of(stream_key, shape, cuts, -0.22, 0.18) * result
    return jnp.clip(result, min=-reach, max=reach).astype(held_as)


def setup_inputs(seed: int = 0) -> dict:
    arg_keys = jax.random.split(jax.random.key(seed), 8)
    displacement = scatter_about(arg_keys[0], (3, GRID_X, GRID_Y, NODES_Z), 1.0, 6.0, ((1, 16), (2, 64)), jnp.float32)
    applied_load = scatter_about(arg_keys[1], (3, GRID_X, GRID_Y, NODES_Z), 1.0, 6.0, ((1, 16), (2, 64)), jnp.float32)
    modulus = jnp.clip(jnp.exp(math.log(3.0) - 2.3025851 * jax.random.uniform(arg_keys[2], (GRID_X, GRID_Y, NODES_Z), jnp.float32) ** steps_of(arg_keys[2], (GRID_X, GRID_Y, NODES_Z), ((0, 16), (1, 64)), -0.2, 0.2)), 0.3, 3.0)
    free_mask = with_ends((jax.random.randint(arg_keys[3], (GRID_X, GRID_Y, NODES_Z), 0, 16) < 15).astype(jnp.int32), jax.random.fold_in(arg_keys[3], 1), 0, 1)
    aggregate_shift = draw_aggregate_shift(jax.random.fold_in(arg_keys[7], 71), 0)
    stencil_table = draw_stencil_table(jax.random.fold_in(arg_keys[7], 71), 0)
    coarse_inverse = draw_coarse_inverse(jax.random.fold_in(arg_keys[7], 71), 0)
    return {"displacement": displacement, "applied_load": applied_load, "modulus": modulus, "free_mask": free_mask, "aggregate_shift": aggregate_shift, "stencil_table": stencil_table, "coarse_inverse": coarse_inverse}


smooth_weight = 0.6
coarse_weight = 0.7


def apply_stencil(bordered, stencil_table, flipped):
    rows_x = bordered.shape[1] - 2
    rows_y = bordered.shape[2] - 2
    depth = bordered.shape[3]
    padded = jnp.pad(bordered, ((0, 0), (0, 0), (0, 0), (1, 1)))
    outputs = [jnp.zeros((rows_x, rows_y, depth), jnp.float32) for comp in range(3)]
    for offset in range(27):
        step_x = offset // 9 - 1
        step_y = (offset // 3) % 3 - 1
        step_z = offset % 3 - 1
        if flipped:
            step_x, step_y, step_z = -step_x, -step_y, -step_z
        windows = [padded[comp, 1 + step_x:1 + step_x + rows_x, 1 + step_y:1 + step_y + rows_y, 1 + step_z:1 + step_z + depth] for comp in range(3)]
        for row in range(3):
            for col in range(3):
                if flipped:
                    factor = stencil_table[offset, col, row]
                else:
                    factor = stencil_table[offset, row, col]
                outputs[row] = outputs[row] + factor * windows[col]
    return jnp.stack(outputs)


def mode_terms(smoothed, shift_code):
    layout = shift_code.shape
    place_x = lax.broadcasted_iota(jnp.int32, layout, 0) % 3 - 1
    place_y = lax.broadcasted_iota(jnp.int32, layout, 1) % 3 - 1
    place_z = lax.broadcasted_iota(jnp.int32, layout, 2) % 3 - 1
    lever_x = (place_x - 3 * (shift_code // 3 - 1)).astype(jnp.float32)
    lever_y = (place_y - 3 * (shift_code % 3 - 1)).astype(jnp.float32)
    lever_z = place_z.astype(jnp.float32)
    push_x, push_y, push_z = smoothed[0], smoothed[1], smoothed[2]
    return jnp.stack([push_x, push_y, push_z,
                      lever_y * push_z - lever_z * push_y,
                      lever_z * push_x - lever_x * push_z,
                      lever_x * push_y - lever_y * push_x])


def collect_blocks(terms, shift_code):
    blocks_x = shift_code.shape[0] // 3
    blocks_y = shift_code.shape[1] // 3
    blocks_z = shift_code.shape[2] // 3
    extended = jnp.zeros((6, blocks_x + 2, blocks_y + 2, blocks_z), jnp.float32)
    for code in range(9):
        shift_x = code // 3 - 1
        shift_y = code % 3 - 1
        picked = jnp.where(shift_code[None] == code, terms, 0.0)
        summed = picked.reshape(6, blocks_x, 3, blocks_y, 3, blocks_z, 3).sum(axis=(2, 4, 6))
        extended = extended.at[:, 1 + shift_x:1 + shift_x + blocks_x, 1 + shift_y:1 + shift_y + blocks_y].add(summed)
    return extended


def reference(displacement, applied_load, modulus, free_mask, aggregate_shift, stencil_table, coarse_inverse):
    freedom = free_mask.astype(jnp.float32)
    source = freedom[None] * applied_load
    stiffness = freedom * modulus
    diagonal = jnp.diagonal(stencil_table[13]).reshape(3, 1, 1, 1)
    wide_moved = jnp.pad(displacement, ((0, 0), (2, 2), (1, 1), (0, 0)))
    wide_source = jnp.pad(source, ((0, 0), (1, 1), (0, 0), (0, 0)))
    wide_stiff = jnp.pad(stiffness, ((1, 1), (0, 0), (0, 0)))
    layer_count = displacement.shape[1] // 3

    def one_layer(layer_id):
        start_row = (3 * layer_id).astype(jnp.int32)
        moved = lax.dynamic_slice_in_dim(wide_moved, start_row, 7, 1)
        loaded = lax.dynamic_slice_in_dim(wide_source, start_row, 5, 1)
        stiff = lax.dynamic_slice_in_dim(wide_stiff, start_row, 5, 0)
        residual = loaded - stiff[None] * apply_stencil(moved, stencil_table, False)
        scaled = jnp.pad(residual / diagonal, ((0, 0), (0, 0), (1, 1), (0, 0)))
        smoothed = residual[:, 1:4] - smooth_weight * apply_stencil(scaled, stencil_table, True)
        shift_code = lax.dynamic_slice_in_dim(aggregate_shift, start_row, 3, 0)
        return collect_blocks(mode_terms(smoothed, shift_code), shift_code)

    layers = lax.map(one_layer, jnp.arange(layer_count, dtype=jnp.int32))
    from_left = jnp.pad(layers[:-1, :, 2], ((1, 0), (0, 0), (0, 0), (0, 0)))
    from_right = jnp.pad(layers[1:, :, 0], ((0, 1), (0, 0), (0, 0), (0, 0)))
    coarse = (layers[:, :, 1] + from_left + from_right)[:, :, 1:-1]
    coarse = jnp.transpose(coarse, (1, 0, 2, 3))
    return coarse_weight * jnp.sum(coarse_inverse * coarse[None], axis=1)
```

```python
import jax
import jax.numpy as jnp
from jax import lax
from jax.experimental import pallas as pl
from jax.experimental.pallas import tpu as pltpu
from jax.sharding import PartitionSpec as P

smooth_weight = 0.6
coarse_weight = 0.7

ROWS = 32
OWN = 24
DEPTH = 384
SLABS = 11
STIFF = 9
CODE = 10
HALO_ROWS = 56
VMEM_LIMIT = 48 * 1024 * 1024


def slab(index):
    return pl.ds(index * ROWS, ROWS)


def pack_kernel(
    moved_low, moved_high, load_low, load_high, modulus_low, modulus_high, mask_low, mask_high, code_low, code_high,
    low_out, high_out,
):
    sides = (
        (low_out, moved_low, load_low, modulus_low, mask_low, code_low, 0, 0, 0),
        (high_out, moved_high, load_high, modulus_high, mask_high, code_high, 5, 6, 7),
    )
    for out, moved, load, modulus, mask, code, first_moved, first_load, first_code in sides:
        for plane in range(3):
            freedom = mask[plane, pl.ds(first_load, 2), :].astype(jnp.float32)
            for comp in range(3):
                unit = comp * 3 + plane
                out[pl.ds(3 * unit, 3), :] = moved[comp, plane, pl.ds(first_moved, 3), :]
                out[pl.ds(27 + 2 * unit, 2), :] = freedom * load[comp, plane, pl.ds(first_load, 2), :]
            out[pl.ds(45 + 2 * plane, 2), :] = freedom * modulus[plane, pl.ds(first_load, 2), :]
            out[pl.ds(51 + plane, 1), :] = (code[plane, pl.ds(first_code, 1), :] + 1).astype(jnp.float32)
        out[pl.ds(54, 2), :] = jnp.zeros((2, DEPTH), jnp.float32)


def roll_rows(ref, index, value):
    ref[index, 0] = pltpu.roll(value, 1, 0)
    ref[index, 1] = value
    ref[index, 2] = pltpu.roll(value, ROWS - 1, 0)


def stencil_rows(table, start, planes, flipped):
    totals = [[None] * 3 for _ in range(3)]
    for step_x, ref, base in planes:
        for step_y in (-1, 0, 1):
            for col in range(3):
                value = ref[base + col, step_y + 1, pl.ds(start, 8), :]
                for step_z in (-1, 0, 1):
                    offset = 9 * (step_x + 1) + 3 * (step_y + 1) + step_z + 1
                    for row in range(3):
                        entry = (26 - offset) * 9 + col * 3 + row if flipped else offset * 9 + row * 3 + col
                        term = table[entry] * value
                        old = totals[row][step_z + 1]
                        totals[row][step_z + 1] = term if old is None else old + term
    column = lax.broadcasted_iota(jnp.int32, (8, DEPTH), 1)
    outputs = []
    for below, same, above in totals:
        below = jnp.where(column == 0, 0.0, pltpu.roll(below, 1, 1))
        above = jnp.where(column == DEPTH - 1, 0.0, pltpu.roll(above, DEPTH - 1, 1))
        outputs.append(same + below + above)
    return outputs


def partial_kernel(
    table, moved, load, modulus, mask, code, from_low, from_high, low_out, high_out, code_out, wide_moved, source, stiff
):
    gap = jnp.zeros((8, DEPTH), jnp.float32)
    halo = pl.ds(OWN, 8)

    def joined(first, count):
        parts = jnp.zeros((8, DEPTH), jnp.float32)
        row = lax.broadcasted_iota(jnp.int32, (8, DEPTH), 0)
        for step in range(count):
            above = from_high[pl.ds(first + step, 1), :]
            below = from_low[pl.ds(first + step, 1), :]
            parts = jnp.where(row == step, above, parts)
            parts = jnp.where(row == 8 - count + step, below, parts)
        return parts

    del gap
    for plane in range(3):
        freedom = mask[plane].astype(jnp.float32)
        for comp in range(3):
            unit = comp * 3 + plane
            index = plane * 3 + comp
            value = jnp.concatenate([moved[comp, plane], joined(3 * unit, 3)], axis=0)
            roll_rows(wide_moved, index, value)
            source[index, pl.ds(0, OWN), :] = freedom * load[comp, plane]
            source[index, halo, :] = joined(27 + 2 * unit, 2)
            if plane == 0:
                low_out[slab(comp), :] = value
            if plane == 2:
                high_out[slab(comp), :] = value
        stiff[plane, pl.ds(0, OWN), :] = freedom * modulus[plane]
        stiff[plane, halo, :] = joined(45 + 2 * plane, 2)
        out, base = ((low_out, CODE * ROWS), (code_out, 0), (high_out, CODE * ROWS))[plane]
        out[pl.ds(base, OWN), :] = (code[plane] + 1).astype(jnp.float32)
        out[pl.ds(base + OWN, 8), :] = joined(51 + plane, 1)
    low_out[slab(STIFF), :] = stiff[0]
    high_out[slab(STIFF), :] = stiff[2]

    def tile(number, carry):
        start = pl.multiple_of(number * 8, 8)
        for plane in range(3):
            steps = [step for step in (-1, 0, 1) if 0 <= plane + step < 3]
            planes = [(step, wide_moved, 3 * (plane + step)) for step in steps]
            product = stencil_rows(table, start, planes, False)
            factor = stiff[plane, pl.ds(start, 8), :]
            for comp in range(3):
                residual = source[plane * 3 + comp, pl.ds(start, 8), :] - factor * product[comp]
                if plane == 0:
                    low_out[pl.ds((3 + comp) * ROWS + start, 8), :] = residual
                elif plane == 2:
                    high_out[pl.ds((3 + comp) * ROWS + start, 8), :] = residual
                else:
                    low_out[pl.ds((6 + comp) * ROWS + start, 8), :] = residual
                    high_out[pl.ds((6 + comp) * ROWS + start, 8), :] = residual
        return carry

    lax.fori_loop(0, ROWS // 8, tile, 0)


def coarse_kernel(
    table, own_low, own_high, from_low, from_high, code_middle, inverse, update, wide_moved, wide_scaled, residuals,
    sums, reduced,
):
    for index, ref in enumerate((from_low, own_low, own_high, from_high)):
        for comp in range(3):
            roll_rows(wide_moved, index * 3 + comp, ref[slab(comp), :])
    for comp in range(3):
        for place, ref in ((0, from_low), (3, own_low), (6, from_high)):
            residuals[place * 3 + comp] = ref[slab(6 + comp), :]

    def finish(number, carry):
        start = pl.multiple_of(number * 8, 8)
        for place, ref, step, other in (
            (1, from_low, 1, 1), (2, own_low, -1, 0), (4, own_high, 1, 3), (5, from_high, -1, 2)
        ):
            product = stencil_rows(table, start, [(step, wide_moved, other * 3)], False)
            factor = ref[pl.ds(STIFF * ROWS + start, 8), :]
            for comp in range(3):
                partial = ref[pl.ds((3 + comp) * ROWS + start, 8), :]
                residuals[place * 3 + comp, pl.ds(start, 8), :] = partial - factor * product[comp]
        return carry

    lax.fori_loop(0, ROWS // 8, finish, 0)

    for comp in range(3):
        diagonal = table[13 * 9 + comp * 4]
        for place in range(7):
            index = place * 3 + comp
            roll_rows(wide_scaled, index, residuals[index] / diagonal)

    code_refs = (
        (from_low, CODE * ROWS), (own_low, CODE * ROWS), (code_middle, 0), (own_high, CODE * ROWS),
        (from_high, CODE * ROWS),
    )

    def tile(number, carry):
        start = pl.multiple_of(number * 8, 8)
        shape = (8, DEPTH)
        stay = [jnp.zeros(shape, jnp.float32) for _ in range(5)]
        leave = [jnp.zeros(shape, jnp.float32) for _ in range(5)]
        for plane in range(-1, 4):
            planes = [(step, wide_scaled, 3 * (plane + step + 2)) for step in (-1, 0, 1)]
            product = stencil_rows(table, start, planes, True)
            ref, base = code_refs[plane + 1]
            code = ref[pl.ds(base + start, 8), :]
            middle = 3.0 * (1 if plane == -1 else -1 if plane == 3 else 0) + 5.0
            stays = code == middle
            leaves = (code == middle - 1.0) | (code == middle + 1.0)
            arm = float(plane - 1)
            for comp in range(3):
                residual = residuals[3 * (plane + 2) + comp, pl.ds(start, 8), :]
                smoothed = residual - smooth_weight * product[comp]
                for held, chosen in ((stay, stays), (leave, leaves)):
                    picked = jnp.where(chosen, smoothed, 0.0)
                    held[comp] = held[comp] + picked
                    if comp > 0 and arm != 0.0:
                        held[2 + comp] = held[2 + comp] + arm * picked
        row = lax.broadcasted_iota(jnp.int32, shape, 0) + start
        row = jnp.where(row == ROWS - 1, 2, row) % 3
        lever_z = (lax.broadcasted_iota(jnp.int32, shape, 1) % 3 - 1).astype(jnp.float32)
        lever_stay = (row - 1).astype(jnp.float32)
        lever_leave = jnp.where(row == 0, 2.0, jnp.where(row == 2, -2.0, 0.0))
        for held, lever_y, base in ((stay, lever_stay, 0), (leave, lever_leave, 6)):
            push_x, push_y, push_z, armed_y, armed_z = held
            modes = (
                push_x, push_y, push_z,
                lever_y * push_z - lever_z * push_y,
                lever_z * push_x - armed_z,
                armed_y - lever_y * push_x,
            )
            for mode in range(6):
                sums[pl.ds((base + mode) * ROWS + start, 8), :] = modes[mode]
        return carry

    lax.fori_loop(0, ROWS // 8, tile, 0)

    node = lax.broadcasted_iota(jnp.int32, (DEPTH, DEPTH // 3), 0)
    block = lax.broadcasted_iota(jnp.int32, (DEPTH, DEPTH // 3), 1)
    groups = (node // 3 == block).astype(jnp.float32)
    compact = jnp.dot(
        sums[...], groups, preferred_element_type=jnp.float32, precision=lax.Precision.HIGHEST
    )
    for mode in range(12):
        part = compact[mode * ROWS : (mode + 1) * ROWS]
        reduced[mode, pl.ds(8, ROWS), :] = part
        reduced[mode, pl.ds(0, 8), :] = part[ROWS - 8 :]
    coarse = []
    for mode in range(6):
        total = reduced[mode, pl.ds(8, 8, stride=3), :]
        total = total + reduced[mode, pl.ds(9, 8, stride=3), :]
        total = total + reduced[mode, pl.ds(10, 8, stride=3), :]
        total = total + reduced[6 + mode, pl.ds(11, 8, stride=3), :]
        total = total + reduced[6 + mode, pl.ds(7, 8, stride=3), :]
        coarse.append(total)
    for row in range(6):
        result = inverse[row, 0, 0] * coarse[0]
        for col in range(1, 6):
            result = result + inverse[row, col, 0] * coarse[col]
        update[row, 0] = coarse_weight * result


def shifted(low_message, high_message, axis):
    count = lax.axis_size(axis)
    forward = [(i, i + 1) for i in range(count - 1)]
    backward = [(target, source) for source, target in forward]
    return lax.ppermute(high_message, axis, forward), lax.ppermute(low_message, axis, backward)


def local(
    displacement, applied_load, modulus, free_mask, aggregate_shift, stencil_table, coarse_inverse
):
    f32 = jnp.float32
    table = stencil_table.reshape(243)
    vmem = pl.BlockSpec(memory_space=pltpu.VMEM)
    smem = pl.BlockSpec(memory_space=pltpu.SMEM)
    vector_low = pl.BlockSpec((3, 3, 8, DEPTH), lambda i: (0, 0, 0, 0))
    vector_high = pl.BlockSpec((3, 3, 8, DEPTH), lambda i: (0, 0, 2, 0))
    scalar_low = pl.BlockSpec((3, 8, DEPTH), lambda i: (0, 0, 0))
    scalar_high = pl.BlockSpec((3, 8, DEPTH), lambda i: (0, 2, 0))
    halo_block = pl.BlockSpec((HALO_ROWS, DEPTH), lambda i: (0, 0))
    halo_shape = jax.ShapeDtypeStruct((HALO_ROWS, DEPTH), f32)
    low_rows, high_rows = pl.pallas_call(
        pack_kernel,
        grid=(1,),
        in_specs=[vector_low, vector_high] * 2 + [scalar_low, scalar_high] * 3,
        out_specs=(halo_block, halo_block),
        out_shape=(halo_shape, halo_shape),
        name="pack_rows",
    )(
        displacement, displacement, applied_load, applied_load, modulus, modulus, free_mask, free_mask,
        aggregate_shift, aggregate_shift,
    )
    below, above = shifted(low_rows, high_rows, "gy")

    message = jax.ShapeDtypeStruct((SLABS * ROWS, DEPTH), f32)
    low_planes, high_planes, code_middle = pl.pallas_call(
        partial_kernel,
        in_specs=[smem] + [vmem] * 7,
        out_specs=(vmem,) * 3,
        out_shape=(message, message, jax.ShapeDtypeStruct((ROWS, DEPTH), f32)),
        scratch_shapes=[
            pltpu.VMEM((9, 3, ROWS, DEPTH), f32), pltpu.VMEM((9, ROWS, DEPTH), f32), pltpu.VMEM((3, ROWS, DEPTH), f32)
        ],
        compiler_params=pltpu.CompilerParams(vmem_limit_bytes=VMEM_LIMIT),
        name="partial_residual",
    )(table, displacement, applied_load, modulus, free_mask, aggregate_shift, below, above)
    left, right = shifted(low_planes, high_planes, "gx")

    return pl.pallas_call(
        coarse_kernel,
        in_specs=[smem] + [vmem] * 6,
        out_specs=vmem,
        out_shape=jax.ShapeDtypeStruct((6, 1, 8, DEPTH // 3), f32),
        scratch_shapes=[
            pltpu.VMEM((12, 3, ROWS, DEPTH), f32),
            pltpu.VMEM((21, 3, ROWS, DEPTH), f32),
            pltpu.VMEM((21, ROWS, DEPTH), f32),
            pltpu.VMEM((12 * ROWS, DEPTH), f32),
            pltpu.VMEM((12, ROWS + 8, DEPTH // 3), f32),
        ],
        compiler_params=pltpu.CompilerParams(vmem_limit_bytes=VMEM_LIMIT),
        name="coarse_update",
    )(table, low_planes, high_planes, left, right, code_middle, coarse_inverse)


def solution(mesh):
    in_specs = (
        P(None, "gx", "gy", None),
        P(None, "gx", "gy", None),
        P("gx", "gy", None),
        P("gx", "gy", None),
        P("gx", "gy", None),
        P(),
        P(None, None, "gx", "gy", None),
    )
    out_specs = P(None, "gx", "gy", None)
    return jax.shard_map(local, mesh=mesh, in_specs=in_specs, out_specs=out_specs, check_vma=False)
```

```python
import jax
import jax.numpy as jnp
from jax import lax
from jax.experimental import pallas as pl
from jax.experimental.pallas import tpu as pltpu
from jax.sharding import PartitionSpec as P

smooth_weight = 0.6
coarse_weight = 0.7

ROWS = 32
OWN = 24
DEPTH = 384
SLABS = 8
PARTIAL = 3
STIFF = 6
CODE = 7
BESIDE = SLABS * OWN
MODES = BESIDE + SLABS * 4
MESSAGE_ROWS = MODES + 16
GROUP = 16
HALO_ROWS = 56
VMEM_LIMIT = 48 * 1024 * 1024


def slab(index):
    return pl.ds(index * ROWS, ROWS)


def pack_kernel(
    moved_all, load_all, modulus_all, mask_all, code_all, first_out, second_out, low_out, high_out, moved, load, modulus,
    mask, code, semaphores,
):
    copies = []
    for index, (whole, held) in enumerate(
        ((moved_all, moved), (load_all, load), (modulus_all, modulus), (mask_all, mask), (code_all, code))
    ):
        for side, begin in enumerate((0, OWN - 8)):
            rows = pl.ds(begin, 8)
            source = whole.at[:, :, rows, :] if index < 2 else whole.at[:, rows, :]
            copies.append(pltpu.make_async_copy(source, held.at[side], semaphores.at[2 * index + side]))
    for copy in copies:
        copy.start()
    for copy in copies:
        copy.wait()
    sides = (
        (low_out, moved.at[0], load.at[0], modulus.at[0], mask.at[0], code.at[0], 0, 0, 0),
        (high_out, moved.at[1], load.at[1], modulus.at[1], mask.at[1], code.at[1], 5, 6, 7),
    )
    for out, moved, load, modulus, mask, code, first_moved, first_load, first_code in sides:
        for plane in range(3):
            freedom = mask[plane, pl.ds(first_load, 2), :].astype(jnp.float32)
            for comp in range(3):
                unit = comp * 3 + plane
                out[pl.ds(3 * unit, 3), :] = moved[comp, plane, pl.ds(first_moved, 3), :]
                out[pl.ds(27 + 2 * unit, 2), :] = freedom * load[comp, plane, pl.ds(first_load, 2), :]
            out[pl.ds(45 + 2 * plane, 2), :] = freedom * modulus[plane, pl.ds(first_load, 2), :]
            out[pl.ds(51 + plane, 1), :] = (code[plane, pl.ds(first_code, 1), :] + 1).astype(jnp.float32)
        out[pl.ds(54, 2), :] = jnp.zeros((2, DEPTH), jnp.float32)
    send_sides("gy", low_out, high_out, first_out, second_out)


def on_sides(axis, copy):
    even = lax.axis_index(axis) % 2 == 0
    pl.when(even)(lambda: copy(True))
    pl.when(jnp.logical_not(even))(lambda: copy(False))


def send_sides(axis, low, high, first_out, second_out):
    def copy(even):
        first_out[...] = low[...] if even else high[...]
        second_out[...] = high[...] if even else low[...]

    on_sides(axis, copy)


def take_sides(axis, first, second, low_out, high_out):
    def copy(even):
        low_out[...] = first[...] if even else second[...]
        high_out[...] = second[...] if even else first[...]

    on_sides(axis, copy)


def pack_slabs(slabs, modes, out):
    row = lax.broadcasted_iota(jnp.int32, (8, DEPTH), 0)
    near = (row < 2) | (row > 5)
    for index in range(SLABS):
        out[pl.ds(index * OWN, OWN), :] = slabs[pl.ds(index * ROWS, OWN), :]
    for index in range(0, SLABS, 2):
        one = slabs[pl.ds(index * ROWS + OWN, 8), :]
        other = pltpu.roll(slabs[pl.ds((index + 1) * ROWS + OWN, 8), :], 4, 0)
        out[pl.ds(BESIDE + index * 4, 8), :] = jnp.where(near, one, other)
    for mode in range(6):
        out[pl.ds(MODES + mode // 3 * 8, 8), pl.ds(mode % 3 * 128, 128)] = modes[mode]


def unpack_slabs(message, slabs, modes):
    for index in range(SLABS):
        slabs[pl.ds(index * ROWS, OWN), :] = message[pl.ds(index * OWN, OWN), :]
    for index in range(0, SLABS, 2):
        both = message[pl.ds(BESIDE + index * 4, 8), :]
        slabs[pl.ds(index * ROWS + OWN, 8), :] = both
        slabs[pl.ds((index + 1) * ROWS + OWN, 8), :] = pltpu.roll(both, 4, 0)
    for mode in range(6):
        modes[mode] = message[pl.ds(MODES + mode // 3 * 8, 8), pl.ds(mode % 3 * 128, 128)]


def roll_rows(ref, index, value):
    ref[index, 0] = pltpu.roll(value, 1, 0)
    ref[index, 1] = value
    ref[index, 2] = pltpu.roll(value, ROWS - 1, 0)


def stencil_rows(table, start, planes, flipped):
    column = lax.broadcasted_iota(jnp.int32, (GROUP, DEPTH), 1)
    outputs = []
    for row in range(3):
        totals = [None] * 3
        for step_x, ref, base in planes:
            for step_y in (-1, 0, 1):
                for col in range(3):
                    value = ref[base + col, step_y + 1, pl.ds(start, GROUP), :]
                    for step_z in (-1, 0, 1):
                        offset = 9 * (step_x + 1) + 3 * (step_y + 1) + step_z + 1
                        entry = (26 - offset) * 9 + col * 3 + row if flipped else offset * 9 + row * 3 + col
                        term = table[entry] * value
                        old = totals[step_z + 1]
                        totals[step_z + 1] = term if old is None else old + term
        below, same, above = totals
        below = jnp.where(column == 0, 0.0, pltpu.roll(below, 1, 1))
        above = jnp.where(column == DEPTH - 1, 0.0, pltpu.roll(above, DEPTH - 1, 1))
        outputs.append(same + below + above)
    return outputs


def joined(from_low, from_high, first, count):
    rows = jnp.zeros((8, DEPTH), jnp.float32)
    place = lax.broadcasted_iota(jnp.int32, (8, DEPTH), 0)
    for step in range(count):
        rows = jnp.where(place == step, from_high[pl.ds(first + step, 1), :], rows)
        rows = jnp.where(place == 8 - count + step, from_low[pl.ds(first + step, 1), :], rows)
    return rows


def tiles(body):
    def tile(number, carry):
        body(pl.multiple_of(number * GROUP, GROUP))
        return carry

    lax.fori_loop(0, ROWS // GROUP, tile, 0)


def fill_plane(plane, load, modulus, mask, from_low, from_high, source, stiff, index):
    halo = pl.ds(OWN, 8)
    freedom = mask[plane].astype(jnp.float32)
    for comp in range(3):
        source[index * 3 + comp, pl.ds(0, OWN), :] = freedom * load[comp, plane]
        source[index * 3 + comp, halo, :] = joined(from_low, from_high, 27 + 2 * (comp * 3 + plane), 2)
    stiff[pl.ds(0, OWN), :] = freedom * modulus[plane]
    stiff[halo, :] = joined(from_low, from_high, 45 + 2 * plane, 2)


def add_plane(stay, leave, smoothed, code, plane):
    middle = 3.0 * (1 if plane == -1 else -1 if plane == 3 else 0) + 5.0
    stays = code == middle
    leaves = (code == middle - 1.0) | (code == middle + 1.0)
    arm = float(plane - 1)
    for held, chosen in ((stay, stays), (leave, leaves)):
        for comp in range(3):
            picked = jnp.where(chosen, smoothed[comp], 0.0)
            held[comp] = held[comp] + picked
            if comp > 0 and arm != 0.0:
                held[2 + comp] = held[2 + comp] + arm * picked


def put_modes(stay, leave, start, sums):
    shape = (GROUP, DEPTH)
    row = lax.broadcasted_iota(jnp.int32, shape, 0) + start
    row = jnp.where(row == ROWS - 1, 2, row) % 3
    lever_z = (lax.broadcasted_iota(jnp.int32, shape, 1) % 3 - 1).astype(jnp.float32)
    lever_stay = (row - 1).astype(jnp.float32)
    lever_leave = jnp.where(row == 0, 2.0, jnp.where(row == 2, -2.0, 0.0))
    for held, lever_y, base in ((stay, lever_stay, 0), (leave, lever_leave, 6)):
        push_x, push_y, push_z, armed_y, armed_z = held
        modes = (
            push_x, push_y, push_z,
            lever_y * push_z - lever_z * push_y,
            lever_z * push_x - armed_z,
            armed_y - lever_y * push_x,
        )
        for mode in range(6):
            for part in range(3):
                sums[base + mode, part, pl.ds(8 + start, GROUP), :] = modes[mode][:, part * 128 : (part + 1) * 128]


def reduce_modes(sums, joint):
    for mode in range(6):
        for part in range(3):
            sums[6 + mode, part, pl.ds(0, 8), :] = sums[6 + mode, part, pl.ds(ROWS, 8), :]
            total = sums[mode, part, pl.ds(8, 8, stride=3), :]
            total = total + sums[mode, part, pl.ds(9, 8, stride=3), :]
            total = total + sums[mode, part, pl.ds(10, 8, stride=3), :]
            total = total + sums[6 + mode, part, pl.ds(11, 8, stride=3), :]
            total = total + sums[6 + mode, part, pl.ds(7, 8, stride=3), :]
            joint[pl.ds(mode * 8, 8), pl.ds(part * 128, 128)] = total
    node = lax.broadcasted_iota(jnp.int32, (DEPTH, DEPTH // 3), 0)
    block = lax.broadcasted_iota(jnp.int32, (DEPTH, DEPTH // 3), 1)
    groups = (node // 3 == block).astype(jnp.bfloat16)
    rest = joint[...]
    compact = jnp.zeros((48, DEPTH // 3), jnp.float32)
    for _ in range(3):
        part = rest.astype(jnp.bfloat16)
        rest = rest - part.astype(jnp.float32)
        compact = compact + jnp.dot(part, groups, preferred_element_type=jnp.float32)
    return [compact[8 * mode : 8 * mode + 8] for mode in range(6)]


def partial_kernel(
    table, moved, load, modulus, mask, code, first, second, first_out, second_out, low_out, high_out, middle_out,
    code_out, early_out, from_low, from_high, wide_moved, source, stiff, wide_scaled, sums, joint, low_modes,
    high_modes,
):
    take_sides("gy", first, second, from_low, from_high)
    for plane in range(3):
        for comp in range(3):
            halo = joined(from_low, from_high, 3 * (comp * 3 + plane), 3)
            roll_rows(wide_moved, plane * 3 + comp, jnp.concatenate([moved[comp, plane], halo], axis=0))
        out = (low_out.at[slab(STIFF)], stiff, high_out.at[slab(STIFF)])[plane]
        fill_plane(plane, load, modulus, mask, from_low, from_high, source, out, plane)
        out, base = ((low_out, CODE * ROWS), (code_out, 0), (high_out, CODE * ROWS))[plane]
        out[pl.ds(base, OWN), :] = (code[plane] + 1).astype(jnp.float32)
        out[pl.ds(base + OWN, 8), :] = joined(from_low, from_high, 51 + plane, 1)

    def body(start):
        for plane in range(-1, 4):
            planes = [(other - plane, wide_moved, 3 * other) for other in range(3) if abs(other - plane) < 2]
            product = stencil_rows(table, start, planes, False)
            out = low_out if plane < 2 else high_out
            if plane in (-1, 3):
                for comp in range(3):
                    out[pl.ds(comp * ROWS + start, GROUP), :] = product[comp]
                continue
            factor = stiff[pl.ds(start, GROUP), :] if plane == 1 else out[pl.ds(STIFF * ROWS + start, GROUP), :]
            for comp in range(3):
                loaded = source[plane * 3 + comp, pl.ds(start, GROUP), :]
                residual = loaded - factor * product[comp]
                if plane == 1:
                    middle_out[pl.ds(comp * ROWS + start, GROUP), :] = residual
                else:
                    out[pl.ds((PARTIAL + comp) * ROWS + start, GROUP), :] = residual

    tiles(body)
    for comp in range(3):
        roll_rows(wide_scaled, comp, middle_out[slab(comp), :] / table[13 * 9 + comp * 4])
    for place, (plane, step, out, modes) in enumerate(((3, 1, low_out, low_modes), (-1, -1, high_out, high_modes))):

        def middle_part(start, place=place, plane=plane, step=step, out=out):
            product = stencil_rows(table, start, [(step, wide_scaled, 0)], True)
            for comp in range(3):
                early_out[pl.ds((place * 3 + comp) * ROWS + start, GROUP), :] = product[comp]
            stay, leave = ([jnp.zeros((GROUP, DEPTH), jnp.float32) for _ in range(5)] for _ in range(2))
            smoothed = [-smooth_weight * product[comp] for comp in range(3)]
            add_plane(stay, leave, smoothed, out[pl.ds(CODE * ROWS + start, GROUP), :], plane)
            put_modes(stay, leave, start, sums)

        tiles(middle_part)
        for mode, value in enumerate(reduce_modes(sums, joint)):
            modes[mode] = value

    def copy(even):
        pack_slabs(low_out, low_modes, first_out if even else second_out)
        pack_slabs(high_out, high_modes, second_out if even else first_out)

    on_sides("gx", copy)


def early_kernel(table, middle, early_out, wide_scaled):
    for comp in range(3):
        roll_rows(wide_scaled, comp, middle[slab(comp), :] / table[13 * 9 + comp * 4])

    def body(start):
        product = stencil_rows(table, start, [(0, wide_scaled, 0)], True)
        for comp in range(3):
            early_out[pl.ds(comp * ROWS + start, GROUP), :] = product[comp]

    tiles(body)


def coarse_kernel(
    table, own_low, own_high, first, second, middle, code_middle, early_outer, early_middle, inverse, update, from_low,
    from_high, residuals, wide_scaled, sums, joint, low_modes, high_modes,
):
    def copy(even):
        unpack_slabs(first if even else second, from_low, low_modes)
        unpack_slabs(second if even else first, from_high, high_modes)

    on_sides("gx", copy)
    places = {-1: 0, 0: 1, 2: 2, 3: 3}
    for comp in range(3):
        diagonal = table[13 * 9 + comp * 4]
        for plane, ref, other in (
            (-1, from_low, own_low), (0, own_low, from_low), (2, own_high, from_high), (3, from_high, own_high)
        ):
            place = places[plane] * 3 + comp
            residual = ref[slab(PARTIAL + comp), :] - ref[slab(STIFF), :] * other[slab(comp), :]
            residuals[place] = residual
            roll_rows(wide_scaled, place, residual / diagonal)

    codes = (
        (from_low, CODE * ROWS), (own_low, CODE * ROWS), (code_middle, 0), (own_high, CODE * ROWS),
        (from_high, CODE * ROWS),
    )

    def body(start):
        shape = (GROUP, DEPTH)
        stay = [jnp.zeros(shape, jnp.float32) for _ in range(5)]
        leave = [jnp.zeros(shape, jnp.float32) for _ in range(5)]
        for plane in range(-1, 4):
            near = [other for other in places if abs(other - plane) < 2]
            planes = [(other - plane, wide_scaled, 3 * places[other]) for other in near]
            product = stencil_rows(table, start, planes, True)
            smoothed = []
            for comp in range(3):
                if plane == 1:
                    residual = middle[pl.ds(comp * ROWS + start, GROUP), :]
                else:
                    residual = residuals[places[plane] * 3 + comp, pl.ds(start, GROUP), :]
                total = product[comp]
                if plane == 1:
                    total = total + early_middle[pl.ds(comp * ROWS + start, GROUP), :]
                elif plane in (0, 2):
                    total = total + early_outer[pl.ds((plane // 2 * 3 + comp) * ROWS + start, GROUP), :]
                smoothed.append(residual - smooth_weight * total)
            ref, base = codes[plane + 1]
            add_plane(stay, leave, smoothed, ref[pl.ds(base + start, GROUP), :], plane)
        put_modes(stay, leave, start, sums)

    tiles(body)
    coarse = [
        value + (low_modes[mode] + high_modes[mode]) for mode, value in enumerate(reduce_modes(sums, joint))
    ]
    for row in range(6):
        result = inverse[row, 0, 0] * coarse[0]
        for col in range(1, 6):
            result = result + inverse[row, col, 0] * coarse[col]
        update[row, 0] = coarse_weight * result


def exchanged(first, second, axis):
    count = lax.axis_size(axis)
    results = []
    for message, begin in ((first, 1), (second, 0)):
        pairs = [pair for i in range(begin, count - 1, 2) for pair in ((i, i + 1), (i + 1, i))]
        results.append(lax.ppermute(message, axis, pairs))
    return results


def local(
    displacement, applied_load, modulus, free_mask, aggregate_shift, stencil_table, coarse_inverse
):
    f32 = jnp.float32
    table = stencil_table.reshape(243)
    vmem = pl.BlockSpec(memory_space=pltpu.VMEM)
    smem = pl.BlockSpec(memory_space=pltpu.SMEM)
    halo_shape = jax.ShapeDtypeStruct((HALO_ROWS, DEPTH), f32)
    first_rows, second_rows = pl.pallas_call(
        pack_kernel,
        in_specs=[pl.BlockSpec(memory_space=pltpu.HBM)] * 5,
        out_specs=(vmem,) * 2,
        out_shape=(halo_shape,) * 2,
        scratch_shapes=[pltpu.VMEM((HALO_ROWS, DEPTH), f32)] * 2
        + [pltpu.VMEM((2, 3, 3, 8, DEPTH), f32)] * 2
        + [pltpu.VMEM((2, 3, 8, DEPTH), f32)]
        + [pltpu.VMEM((2, 3, 8, DEPTH), jnp.int32)] * 2
        + [pltpu.SemaphoreType.DMA((10,))],
        compiler_params=pltpu.CompilerParams(vmem_limit_bytes=56300000),
        name="pack_rows",
    )(displacement, applied_load, modulus, free_mask, aggregate_shift)
    first_rows, second_rows = exchanged(first_rows, second_rows, "gy")

    def rows_of(slabs):
        return jax.ShapeDtypeStruct((slabs * ROWS, DEPTH), f32)

    def held(*shape):
        return pltpu.VMEM(shape + (DEPTH,), f32)

    params = pltpu.CompilerParams(vmem_limit_bytes=VMEM_LIMIT)
    sums = pltpu.VMEM((12, 3, ROWS + 8, 128), f32)
    modes = pltpu.VMEM((6, 8, DEPTH // 3), f32)
    message = jax.ShapeDtypeStruct((MESSAGE_ROWS, DEPTH), f32)
    first_planes, second_planes, low_planes, high_planes, middle, code_middle, early_outer = pl.pallas_call(
        partial_kernel,
        in_specs=[smem] + [vmem] * 7,
        out_specs=(vmem,) * 7,
        out_shape=(message,) * 2 + (rows_of(SLABS),) * 2 + (rows_of(3), rows_of(1), rows_of(6)),
        scratch_shapes=[
            held(HALO_ROWS), held(HALO_ROWS), held(9, 3, ROWS), held(9, ROWS), held(ROWS), held(3, 3, ROWS),
            sums, held(48), modes, modes,
        ],
        compiler_params=params,
        name="partial_residual",
    )(table, displacement, applied_load, modulus, free_mask, aggregate_shift, first_rows, second_rows)
    first_planes, second_planes = exchanged(first_planes, second_planes, "gx")

    early_middle = pl.pallas_call(
        early_kernel,
        in_specs=[smem, vmem],
        out_specs=vmem,
        out_shape=rows_of(3),
        scratch_shapes=[held(3, 3, ROWS)],
        compiler_params=params,
        name="early_product",
    )(table, middle)

    return pl.pallas_call(
        coarse_kernel,
        in_specs=[smem] + [vmem] * 9,
        out_specs=vmem,
        out_shape=jax.ShapeDtypeStruct((6, 1, 8, DEPTH // 3), f32),
        scratch_shapes=[
            held(SLABS * ROWS), held(SLABS * ROWS), held(12, ROWS), held(12, 3, ROWS), sums, held(48), modes,
            modes,
        ],
        compiler_params=params,
        name="coarse_update",
    )(
        table, low_planes, high_planes, first_planes, second_planes, middle, code_middle, early_outer, early_middle,
        coarse_inverse,
    )


def solution(mesh):
    in_specs = (
        P(None, "gx", "gy", None),
        P(None, "gx", "gy", None),
        P("gx", "gy", None),
        P("gx", "gy", None),
        P("gx", "gy", None),
        P(),
        P(None, None, "gx", "gy", None),
    )
    out_specs = P(None, "gx", "gy", None)
    return jax.shard_map(local, mesh=mesh, in_specs=in_specs, out_specs=out_specs, check_vma=False)
```

```python
import jax
import jax.numpy as jnp
from jax import lax
from jax.experimental import pallas as pl
from jax.experimental.pallas import tpu as pltpu
from jax.sharding import PartitionSpec as P

smooth_weight = 0.6
coarse_weight = 0.7

ROWS = 32
OWN = 24
DEPTH = 384
SLABS = 8
PARTIAL = 3
STIFF = 6
CODE = 7
BESIDE = SLABS * OWN
MODES = BESIDE + SLABS * 4
MESSAGE_ROWS = MODES + 16
GROUP = 32
HALO_ROWS = 56
VMEM_LIMIT = 48 * 1024 * 1024


def slab(index):
    return pl.ds(index * ROWS, ROWS)


def pack_kernel(
    moved_all, load_all, modulus_all, mask_all, code_all, first_out, second_out, low_out, high_out, moved, load, modulus,
    mask, code, semaphores,
):
    copies = []
    for index, (whole, held) in enumerate(
        ((moved_all, moved), (load_all, load), (modulus_all, modulus), (mask_all, mask), (code_all, code))
    ):
        for side, begin in enumerate((0, OWN - 8)):
            rows = pl.ds(begin, 8)
            source = whole.at[:, :, rows, :] if index < 2 else whole.at[:, rows, :]
            copies.append(pltpu.make_async_copy(source, held.at[side], semaphores.at[2 * index + side]))
    for copy in copies:
        copy.start()
    for copy in copies:
        copy.wait()
    sides = (
        (low_out, moved.at[0], load.at[0], modulus.at[0], mask.at[0], code.at[0], 0, 0, 0),
        (high_out, moved.at[1], load.at[1], modulus.at[1], mask.at[1], code.at[1], 5, 6, 7),
    )
    for out, moved, load, modulus, mask, code, first_moved, first_load, first_code in sides:
        for plane in range(3):
            freedom = mask[plane, pl.ds(first_load, 2), :].astype(jnp.float32)
            for comp in range(3):
                unit = comp * 3 + plane
                out[pl.ds(3 * unit, 3), :] = moved[comp, plane, pl.ds(first_moved, 3), :]
                out[pl.ds(27 + 2 * unit, 2), :] = freedom * load[comp, plane, pl.ds(first_load, 2), :]
            out[pl.ds(45 + 2 * plane, 2), :] = freedom * modulus[plane, pl.ds(first_load, 2), :]
            out[pl.ds(51 + plane, 1), :] = (code[plane, pl.ds(first_code, 1), :] + 1).astype(jnp.float32)
        out[pl.ds(54, 2), :] = jnp.zeros((2, DEPTH), jnp.float32)
    send_sides("gy", low_out, high_out, first_out, second_out)


def on_sides(axis, copy):
    even = lax.axis_index(axis) % 2 == 0
    pl.when(even)(lambda: copy(True))
    pl.when(jnp.logical_not(even))(lambda: copy(False))


def send_sides(axis, low, high, first_out, second_out):
    def copy(even):
        first_out[...] = low[...] if even else high[...]
        second_out[...] = high[...] if even else low[...]

    on_sides(axis, copy)


def take_sides(axis, first, second, low_out, high_out):
    def copy(even):
        low_out[...] = first[...] if even else second[...]
        high_out[...] = second[...] if even else first[...]

    on_sides(axis, copy)


def pack_slabs(slabs, modes, out):
    row = lax.broadcasted_iota(jnp.int32, (8, DEPTH), 0)
    near = (row < 2) | (row > 5)
    for index in range(SLABS):
        out[pl.ds(index * OWN, OWN), :] = slabs[pl.ds(index * ROWS, OWN), :]
    for index in range(0, SLABS, 2):
        one = slabs[pl.ds(index * ROWS + OWN, 8), :]
        other = pltpu.roll(slabs[pl.ds((index + 1) * ROWS + OWN, 8), :], 4, 0)
        out[pl.ds(BESIDE + index * 4, 8), :] = jnp.where(near, one, other)
    for mode in range(6):
        out[pl.ds(MODES + mode // 3 * 8, 8), pl.ds(mode % 3 * 128, 128)] = modes[mode]


def unpack_slabs(message, slabs, modes):
    for index in range(SLABS):
        slabs[pl.ds(index * ROWS, OWN), :] = message[pl.ds(index * OWN, OWN), :]
    for index in range(0, SLABS, 2):
        both = message[pl.ds(BESIDE + index * 4, 8), :]
        slabs[pl.ds(index * ROWS + OWN, 8), :] = both
        slabs[pl.ds((index + 1) * ROWS + OWN, 8), :] = pltpu.roll(both, 4, 0)
    for mode in range(6):
        modes[mode] = message[pl.ds(MODES + mode // 3 * 8, 8), pl.ds(mode % 3 * 128, 128)]


def roll_rows(ref, index, value):
    ref[index, 0] = pltpu.roll(value, 1, 0)
    ref[index, 1] = value
    ref[index, 2] = pltpu.roll(value, ROWS - 1, 0)


def stencil_rows(table, start, planes, flipped):
    column = lax.broadcasted_iota(jnp.int32, (GROUP, DEPTH), 1)
    outputs = []
    for row in range(3):
        totals = [None] * 3
        for step_x, ref, base in planes:
            for step_y in (-1, 0, 1):
                for col in range(3):
                    value = ref[base + col, step_y + 1, pl.ds(start, GROUP), :]
                    for step_z in (-1, 0, 1):
                        offset = 9 * (step_x + 1) + 3 * (step_y + 1) + step_z + 1
                        entry = (26 - offset) * 9 + col * 3 + row if flipped else offset * 9 + row * 3 + col
                        term = table[entry] * value
                        old = totals[step_z + 1]
                        totals[step_z + 1] = term if old is None else old + term
        below, same, above = totals
        below = jnp.where(column == 0, 0.0, pltpu.roll(below, 1, 1))
        above = jnp.where(column == DEPTH - 1, 0.0, pltpu.roll(above, DEPTH - 1, 1))
        outputs.append(same + below + above)
    return outputs


def joined(from_low, from_high, first, count):
    rows = jnp.zeros((8, DEPTH), jnp.float32)
    place = lax.broadcasted_iota(jnp.int32, (8, DEPTH), 0)
    for step in range(count):
        rows = jnp.where(place == step, from_high[pl.ds(first + step, 1), :], rows)
        rows = jnp.where(place == 8 - count + step, from_low[pl.ds(first + step, 1), :], rows)
    return rows


def tiles(body):
    for start in range(0, ROWS, GROUP):
        body(start)


def fill_plane(plane, load, modulus, mask, from_low, from_high, source, stiff, index):
    halo = pl.ds(OWN, 8)
    freedom = mask[plane].astype(jnp.float32)
    for comp in range(3):
        source[index * 3 + comp, pl.ds(0, OWN), :] = freedom * load[comp, plane]
        source[index * 3 + comp, halo, :] = joined(from_low, from_high, 27 + 2 * (comp * 3 + plane), 2)
    stiff[pl.ds(0, OWN), :] = freedom * modulus[plane]
    stiff[halo, :] = joined(from_low, from_high, 45 + 2 * plane, 2)


def add_plane(stay, leave, smoothed, code, plane):
    middle = 3.0 * (1 if plane == -1 else -1 if plane == 3 else 0) + 5.0
    stays = code == middle
    leaves = (code == middle - 1.0) | (code == middle + 1.0)
    arm = float(plane - 1)
    for held, chosen in ((stay, stays), (leave, leaves)):
        for comp in range(3):
            picked = jnp.where(chosen, smoothed[comp], 0.0)
            held[comp] = held[comp] + picked
            if comp > 0 and arm != 0.0:
                held[2 + comp] = held[2 + comp] + arm * picked


def put_modes(stay, leave, start, sums):
    shape = (GROUP, DEPTH)
    row = lax.broadcasted_iota(jnp.int32, shape, 0) + start
    row = jnp.where(row == ROWS - 1, 2, row) % 3
    lever_z = (lax.broadcasted_iota(jnp.int32, shape, 1) % 3 - 1).astype(jnp.float32)
    lever_stay = (row - 1).astype(jnp.float32)
    lever_leave = jnp.where(row == 0, 2.0, jnp.where(row == 2, -2.0, 0.0))
    for held, lever_y, base in ((stay, lever_stay, 0), (leave, lever_leave, 6)):
        push_x, push_y, push_z, armed_y, armed_z = held
        modes = (
            push_x, push_y, push_z,
            lever_y * push_z - lever_z * push_y,
            lever_z * push_x - armed_z,
            armed_y - lever_y * push_x,
        )
        for mode in range(6):
            for part in range(3):
                sums[base + mode, part, pl.ds(8 + start, GROUP), :] = modes[mode][:, part * 128 : (part + 1) * 128]


def reduce_modes(sums, joint):
    for mode in range(6):
        for part in range(3):
            sums[6 + mode, part, pl.ds(0, 8), :] = sums[6 + mode, part, pl.ds(ROWS, 8), :]
            total = sums[mode, part, pl.ds(8, 8, stride=3), :]
            total = total + sums[mode, part, pl.ds(9, 8, stride=3), :]
            total = total + sums[mode, part, pl.ds(10, 8, stride=3), :]
            total = total + sums[6 + mode, part, pl.ds(11, 8, stride=3), :]
            total = total + sums[6 + mode, part, pl.ds(7, 8, stride=3), :]
            joint[pl.ds(mode * 8, 8), pl.ds(part * 128, 128)] = total
    node = lax.broadcasted_iota(jnp.int32, (DEPTH, DEPTH // 3), 0)
    block = lax.broadcasted_iota(jnp.int32, (DEPTH, DEPTH // 3), 1)
    groups = (node // 3 == block).astype(jnp.bfloat16)
    rest = joint[...]
    compact = jnp.zeros((48, DEPTH // 3), jnp.float32)
    for _ in range(3):
        part = rest.astype(jnp.bfloat16)
        rest = rest - part.astype(jnp.float32)
        compact = compact + jnp.dot(part, groups, preferred_element_type=jnp.float32)
    return [compact[8 * mode : 8 * mode + 8] for mode in range(6)]


def partial_kernel(
    table, moved, load, modulus, mask, code, first, second, first_out, second_out, low_out, high_out, middle_out,
    code_out, early_out, from_low, from_high, wide_moved, source, stiff, wide_scaled, sums, joint, low_modes,
    high_modes,
):
    take_sides("gy", first, second, from_low, from_high)
    for plane in range(3):
        for comp in range(3):
            halo = joined(from_low, from_high, 3 * (comp * 3 + plane), 3)
            roll_rows(wide_moved, plane * 3 + comp, jnp.concatenate([moved[comp, plane], halo], axis=0))
        out = (low_out.at[slab(STIFF)], stiff, high_out.at[slab(STIFF)])[plane]
        fill_plane(plane, load, modulus, mask, from_low, from_high, source, out, plane)
        out, base = ((low_out, CODE * ROWS), (code_out, 0), (high_out, CODE * ROWS))[plane]
        out[pl.ds(base, OWN), :] = (code[plane] + 1).astype(jnp.float32)
        out[pl.ds(base + OWN, 8), :] = joined(from_low, from_high, 51 + plane, 1)

    def body(start):
        for plane in range(-1, 4):
            planes = [(other - plane, wide_moved, 3 * other) for other in range(3) if abs(other - plane) < 2]
            product = stencil_rows(table, start, planes, False)
            out = low_out if plane < 2 else high_out
            if plane in (-1, 3):
                for comp in range(3):
                    out[pl.ds(comp * ROWS + start, GROUP), :] = product[comp]
                continue
            factor = stiff[pl.ds(start, GROUP), :] if plane == 1 else out[pl.ds(STIFF * ROWS + start, GROUP), :]
            for comp in range(3):
                loaded = source[plane * 3 + comp, pl.ds(start, GROUP), :]
                residual = loaded - factor * product[comp]
                if plane == 1:
                    middle_out[pl.ds(comp * ROWS + start, GROUP), :] = residual
                else:
                    out[pl.ds((PARTIAL + comp) * ROWS + start, GROUP), :] = residual

    tiles(body)
    for comp in range(3):
        roll_rows(wide_scaled, comp, middle_out[slab(comp), :] / table[13 * 9 + comp * 4])
    for place, (plane, step, out, modes) in enumerate(((3, 1, low_out, low_modes), (-1, -1, high_out, high_modes))):

        def middle_part(start, place=place, plane=plane, step=step, out=out):
            product = stencil_rows(table, start, [(step, wide_scaled, 0)], True)
            for comp in range(3):
                early_out[pl.ds((place * 3 + comp) * ROWS + start, GROUP), :] = product[comp]
            stay, leave = ([jnp.zeros((GROUP, DEPTH), jnp.float32) for _ in range(5)] for _ in range(2))
            smoothed = [-smooth_weight * product[comp] for comp in range(3)]
            add_plane(stay, leave, smoothed, out[pl.ds(CODE * ROWS + start, GROUP), :], plane)
            put_modes(stay, leave, start, sums)

        tiles(middle_part)
        for mode, value in enumerate(reduce_modes(sums, joint)):
            modes[mode] = value

    def copy(even):
        pack_slabs(low_out, low_modes, first_out if even else second_out)
        pack_slabs(high_out, high_modes, second_out if even else first_out)

    on_sides("gx", copy)


def finish_side(table, message, own, residuals, wide_scaled):
    for comp in range(3):
        diagonal = table[13 * 9 + comp * 4]
        for place, (ref, other) in enumerate(((message, own), (own, message))):
            residual = ref[slab(PARTIAL + comp), :] - ref[slab(STIFF), :] * other[slab(comp), :]
            residuals[place * 3 + comp] = residual
            roll_rows(wide_scaled, place * 3 + comp, residual / diagonal)


def side_product(table, start, plane, near, low, wide_scaled):
    sign = 1 if low else -1
    return stencil_rows(table, start, [(sign * (other - plane), wide_scaled, 3 * (other + 1)) for other in near], True)


def add_side(table, start, stay, leave, message, own, early_outer, low, residuals, wide_scaled):
    for plane, ref in ((-1, message), (0, own)):
        product = side_product(table, start, plane, (-1, 0), low, wide_scaled)
        smoothed = []
        for comp in range(3):
            total = product[comp]
            if plane == 0:
                total = total + early_outer[pl.ds(((0 if low else 3) + comp) * ROWS + start, GROUP), :]
            smoothed.append(residuals[(plane + 1) * 3 + comp, pl.ds(start, GROUP), :] - smooth_weight * total)
        code = ref[pl.ds(CODE * ROWS + start, GROUP), :]
        add_plane(stay, leave, smoothed, code, plane if low else 2 - plane)


def first_side_kernel(
    table, own_low, own_high, first, middle, early_outer, held_out, product_out, modes_out, message, residuals,
    wide_scaled, scaled_middle,
):
    for comp in range(3):
        roll_rows(scaled_middle, comp, middle[slab(comp), :] / table[13 * 9 + comp * 4])

    def side(low):
        own = own_low if low else own_high
        unpack_slabs(first, message, modes_out)
        finish_side(table, message, own, residuals, wide_scaled)

        def body(start):
            stay, leave = ([jnp.zeros((GROUP, DEPTH), jnp.float32) for _ in range(5)] for _ in range(2))
            add_side(table, start, stay, leave, message, own, early_outer, low, residuals, wide_scaled)
            for index, value in enumerate(stay + leave):
                held_out[pl.ds(index * ROWS + start, GROUP), :] = value
            step = -1 if low else 1
            product = stencil_rows(table, start, [(step, wide_scaled, 3), (0, scaled_middle, 0)], True)
            for comp in range(3):
                product_out[pl.ds(comp * ROWS + start, GROUP), :] = product[comp]

        tiles(body)

    on_sides("gx", side)


def coarse_kernel(
    table, own_low, own_high, second, middle, code_middle, early_outer, begun, begun_product, begun_modes, inverse,
    update, message, residuals, wide_scaled, sums, joint, modes,
):
    def side(first_low):
        low = not first_low
        own = own_low if low else own_high
        unpack_slabs(second, message, modes)
        finish_side(table, message, own, residuals, wide_scaled)

        def body(start):
            stay = [begun[pl.ds(index * ROWS + start, GROUP), :] for index in range(5)]
            leave = [begun[pl.ds((5 + index) * ROWS + start, GROUP), :] for index in range(5)]
            add_side(table, start, stay, leave, message, own, early_outer, low, residuals, wide_scaled)
            product = side_product(table, start, 1, (0,), low, wide_scaled)
            smoothed = []
            for comp in range(3):
                rows = pl.ds(comp * ROWS + start, GROUP)
                total = product[comp] + begun_product[rows, :]
                smoothed.append(middle[rows, :] - smooth_weight * total)
            add_plane(stay, leave, smoothed, code_middle[pl.ds(start, GROUP), :], 1)
            put_modes(stay, leave, start, sums)

        tiles(body)

    on_sides("gx", side)
    coarse = [
        value + (begun_modes[mode] + modes[mode]) for mode, value in enumerate(reduce_modes(sums, joint))
    ]
    for row in range(6):
        result = inverse[row, 0, 0] * coarse[0]
        for col in range(1, 6):
            result = result + inverse[row, col, 0] * coarse[col]
        update[row, 0] = coarse_weight * result


def exchanged(first, second, axis):
    count = lax.axis_size(axis)
    results = []
    for message, begin in ((first, 1), (second, 0)):
        pairs = [pair for i in range(begin, count - 1, 2) for pair in ((i, i + 1), (i + 1, i))]
        results.append(lax.ppermute(message, axis, pairs))
    return results


def local(
    displacement, applied_load, modulus, free_mask, aggregate_shift, stencil_table, coarse_inverse
):
    f32 = jnp.float32
    table = stencil_table.reshape(243)
    vmem = pl.BlockSpec(memory_space=pltpu.VMEM)
    smem = pl.BlockSpec(memory_space=pltpu.SMEM)
    halo_shape = jax.ShapeDtypeStruct((HALO_ROWS, DEPTH), f32)
    first_rows, second_rows = pl.pallas_call(
        pack_kernel,
        in_specs=[pl.BlockSpec(memory_space=pltpu.HBM)] * 5,
        out_specs=(vmem,) * 2,
        out_shape=(halo_shape,) * 2,
        scratch_shapes=[pltpu.VMEM((HALO_ROWS, DEPTH), f32)] * 2
        + [pltpu.VMEM((2, 3, 3, 8, DEPTH), f32)] * 2
        + [pltpu.VMEM((2, 3, 8, DEPTH), f32)]
        + [pltpu.VMEM((2, 3, 8, DEPTH), jnp.int32)] * 2
        + [pltpu.SemaphoreType.DMA((10,))],
        compiler_params=pltpu.CompilerParams(vmem_limit_bytes=56300000),
        name="pack_rows",
    )(displacement, applied_load, modulus, free_mask, aggregate_shift)
    first_rows, second_rows = exchanged(first_rows, second_rows, "gy")

    def rows_of(slabs):
        return jax.ShapeDtypeStruct((slabs * ROWS, DEPTH), f32)

    def held(*shape):
        return pltpu.VMEM(shape + (DEPTH,), f32)

    params = pltpu.CompilerParams(vmem_limit_bytes=VMEM_LIMIT)
    sums = pltpu.VMEM((12, 3, ROWS + 8, 128), f32)
    modes = pltpu.VMEM((6, 8, DEPTH // 3), f32)
    message = jax.ShapeDtypeStruct((MESSAGE_ROWS, DEPTH), f32)
    first_planes, second_planes, low_planes, high_planes, middle, code_middle, early_outer = pl.pallas_call(
        partial_kernel,
        in_specs=[smem] + [vmem] * 7,
        out_specs=(vmem,) * 7,
        out_shape=(message,) * 2 + (rows_of(SLABS),) * 2 + (rows_of(3), rows_of(1), rows_of(6)),
        scratch_shapes=[
            held(HALO_ROWS), held(HALO_ROWS), held(9, 3, ROWS), held(9, ROWS), held(ROWS), held(3, 3, ROWS),
            sums, held(48), modes, modes,
        ],
        compiler_params=params,
        name="partial_residual",
    )(table, displacement, applied_load, modulus, free_mask, aggregate_shift, first_rows, second_rows)
    first_planes, second_planes = exchanged(first_planes, second_planes, "gx")

    sides = [held(SLABS * ROWS), held(6, ROWS), held(6, 3, ROWS)]
    begun, begun_product, begun_modes = pl.pallas_call(
        first_side_kernel,
        in_specs=[smem] + [vmem] * 5,
        out_specs=(vmem,) * 3,
        out_shape=(rows_of(10), rows_of(3), jax.ShapeDtypeStruct((6, 8, DEPTH // 3), f32)),
        scratch_shapes=sides + [held(3, 3, ROWS)],
        compiler_params=params,
        name="first_side",
    )(table, low_planes, high_planes, first_planes, middle, early_outer)

    return pl.pallas_call(
        coarse_kernel,
        in_specs=[smem] + [vmem] * 10,
        out_specs=vmem,
        out_shape=jax.ShapeDtypeStruct((6, 1, 8, DEPTH // 3), f32),
        scratch_shapes=sides + [sums, held(48), modes],
        compiler_params=params,
        name="coarse_update",
    )(
        table, low_planes, high_planes, second_planes, middle, code_middle, early_outer, begun, begun_product,
        begun_modes, coarse_inverse,
    )


def solution(mesh):
    in_specs = (
        P(None, "gx", "gy", None),
        P(None, "gx", "gy", None),
        P("gx", "gy", None),
        P("gx", "gy", None),
        P("gx", "gy", None),
        P(),
        P(None, None, "gx", "gy", None),
    )
    out_specs = P(None, "gx", "gy", None)
    return jax.shard_map(local, mesh=mesh, in_specs=in_specs, out_specs=out_specs, check_vma=False)
```

```python
import jax
import jax.numpy as jnp
from jax import lax
from jax.experimental import pallas as pl
from jax.experimental.pallas import tpu as pltpu
from jax.sharding import PartitionSpec as P

smooth_weight = 0.6
coarse_weight = 0.7

ROWS = 32
OWN = 24
DEPTH = 384
SLABS = 8
PARTIAL = 3
STIFF = 6
CODE = 7
BESIDE = SLABS * OWN
MODES = BESIDE + SLABS * 4
MESSAGE_ROWS = MODES + 16
GROUP = 32
HALO_ROWS = 56
VMEM_LIMIT = 48 * 1024 * 1024


def slab(index):
    return pl.ds(index * ROWS, ROWS)


def pack_kernel(
    moved_all, load_all, modulus_all, mask_all, code_all, first_out, second_out, low_out, high_out, moved, load, modulus,
    mask, code, semaphores,
):
    copies = []
    for index, (whole, held) in enumerate(
        ((moved_all, moved), (load_all, load), (modulus_all, modulus), (mask_all, mask), (code_all, code))
    ):
        for side, begin in enumerate((0, OWN - 8)):
            rows = pl.ds(begin, 8)
            source = whole.at[:, :, rows, :] if index < 2 else whole.at[:, rows, :]
            copies.append(pltpu.make_async_copy(source, held.at[side], semaphores.at[2 * index + side]))
    for copy in copies:
        copy.start()
    for copy in copies:
        copy.wait()
    sides = (
        (low_out, moved.at[0], load.at[0], modulus.at[0], mask.at[0], code.at[0], 0, 0, 0),
        (high_out, moved.at[1], load.at[1], modulus.at[1], mask.at[1], code.at[1], 5, 6, 7),
    )
    for out, moved, load, modulus, mask, code, first_moved, first_load, first_code in sides:
        for plane in range(3):
            freedom = mask[plane, pl.ds(first_load, 2), :].astype(jnp.float32)
            for comp in range(3):
                unit = comp * 3 + plane
                out[pl.ds(3 * unit, 3), :] = moved[comp, plane, pl.ds(first_moved, 3), :]
                out[pl.ds(27 + 2 * unit, 2), :] = freedom * load[comp, plane, pl.ds(first_load, 2), :]
            out[pl.ds(45 + 2 * plane, 2), :] = freedom * modulus[plane, pl.ds(first_load, 2), :]
            out[pl.ds(51 + plane, 1), :] = (code[plane, pl.ds(first_code, 1), :] + 1).astype(jnp.float32)
        out[pl.ds(54, 2), :] = jnp.zeros((2, DEPTH), jnp.float32)
    send_sides("gy", low_out, high_out, first_out, second_out)


def on_sides(axis, copy):
    even = lax.axis_index(axis) % 2 == 0
    pl.when(even)(lambda: copy(True))
    pl.when(jnp.logical_not(even))(lambda: copy(False))


def send_sides(axis, low, high, first_out, second_out):
    def copy(even):
        first_out[...] = low[...] if even else high[...]
        second_out[...] = high[...] if even else low[...]

    on_sides(axis, copy)


def take_sides(axis, first, second, low_out, high_out):
    def copy(even):
        low_out[...] = first[...] if even else second[...]
        high_out[...] = second[...] if even else first[...]

    on_sides(axis, copy)


def pack_slabs(slabs, modes, out):
    row = lax.broadcasted_iota(jnp.int32, (8, DEPTH), 0)
    near = (row < 2) | (row > 5)
    for index in range(SLABS):
        out[pl.ds(index * OWN, OWN), :] = slabs[pl.ds(index * ROWS, OWN), :]
    for index in range(0, SLABS, 2):
        one = slabs[pl.ds(index * ROWS + OWN, 8), :]
        other = pltpu.roll(slabs[pl.ds((index + 1) * ROWS + OWN, 8), :], 4, 0)
        out[pl.ds(BESIDE + index * 4, 8), :] = jnp.where(near, one, other)
    for mode in range(6):
        out[pl.ds(MODES + mode // 3 * 8, 8), pl.ds(mode % 3 * 128, 128)] = modes[mode]


def unpack_slabs(message, slabs, modes):
    for index in range(SLABS):
        slabs[pl.ds(index * ROWS, OWN), :] = message[pl.ds(index * OWN, OWN), :]
    for index in range(0, SLABS, 2):
        both = message[pl.ds(BESIDE + index * 4, 8), :]
        slabs[pl.ds(index * ROWS + OWN, 8), :] = both
        slabs[pl.ds((index + 1) * ROWS + OWN, 8), :] = pltpu.roll(both, 4, 0)
    for mode in range(6):
        modes[mode] = message[pl.ds(MODES + mode // 3 * 8, 8), pl.ds(mode % 3 * 128, 128)]


def roll_rows(ref, index, value):
    ref[index, 0] = pltpu.roll(value, 1, 0)
    ref[index, 1] = value
    ref[index, 2] = pltpu.roll(value, ROWS - 1, 0)


def stencil_rows(table, start, planes, flipped):
    column = lax.broadcasted_iota(jnp.int32, (GROUP, DEPTH), 1)
    outputs = []
    for row in range(3):
        totals = [None] * 3
        for step_x, ref, base in planes:
            for step_y in (-1, 0, 1):
                for col in range(3):
                    value = ref[base + col, step_y + 1, pl.ds(start, GROUP), :]
                    for step_z in (-1, 0, 1):
                        offset = 9 * (step_x + 1) + 3 * (step_y + 1) + step_z + 1
                        entry = (26 - offset) * 9 + col * 3 + row if flipped else offset * 9 + row * 3 + col
                        term = table[entry] * value
                        old = totals[step_z + 1]
                        totals[step_z + 1] = term if old is None else old + term
        below, same, above = totals
        below = jnp.where(column == 0, 0.0, pltpu.roll(below, 1, 1))
        above = jnp.where(column == DEPTH - 1, 0.0, pltpu.roll(above, DEPTH - 1, 1))
        outputs.append(same + below + above)
    return outputs


def joined(from_low, from_high, first, count):
    rows = jnp.zeros((8, DEPTH), jnp.float32)
    place = lax.broadcasted_iota(jnp.int32, (8, DEPTH), 0)
    for step in range(count):
        rows = jnp.where(place == step, from_high[pl.ds(first + step, 1), :], rows)
        rows = jnp.where(place == 8 - count + step, from_low[pl.ds(first + step, 1), :], rows)
    return rows


def tiles(body):
    for start in range(0, ROWS, GROUP):
        body(start)


def fill_plane(plane, load, modulus, mask, from_low, from_high, source, stiff, index):
    halo = pl.ds(OWN, 8)
    freedom = mask[plane].astype(jnp.float32)
    for comp in range(3):
        source[index * 3 + comp, pl.ds(0, OWN), :] = freedom * load[comp, plane]
        source[index * 3 + comp, halo, :] = joined(from_low, from_high, 27 + 2 * (comp * 3 + plane), 2)
    stiff[pl.ds(0, OWN), :] = freedom * modulus[plane]
    stiff[halo, :] = joined(from_low, from_high, 45 + 2 * plane, 2)


def add_plane(stay, leave, smoothed, code, plane):
    middle = 3.0 * (1 if plane == -1 else -1 if plane == 3 else 0) + 5.0
    stays = code == middle
    leaves = (code == middle - 1.0) | (code == middle + 1.0)
    arm = float(plane - 1)
    for held, chosen in ((stay, stays), (leave, leaves)):
        for comp in range(3):
            picked = jnp.where(chosen, smoothed[comp], 0.0)
            held[comp] = held[comp] + picked
            if comp > 0 and arm != 0.0:
                held[2 + comp] = held[2 + comp] + arm * picked


def put_modes(stay, leave, start, sums):
    shape = (GROUP, DEPTH)
    row = lax.broadcasted_iota(jnp.int32, shape, 0) + start
    row = jnp.where(row == ROWS - 1, 2, row) % 3
    lever_z = (lax.broadcasted_iota(jnp.int32, shape, 1) % 3 - 1).astype(jnp.float32)
    lever_stay = (row - 1).astype(jnp.float32)
    lever_leave = jnp.where(row == 0, 2.0, jnp.where(row == 2, -2.0, 0.0))
    for held, lever_y, base in ((stay, lever_stay, 0), (leave, lever_leave, 6)):
        push_x, push_y, push_z, armed_y, armed_z = held
        modes = (
            push_x, push_y, push_z,
            lever_y * push_z - lever_z * push_y,
            lever_z * push_x - armed_z,
            armed_y - lever_y * push_x,
        )
        for mode in range(6):
            for part in range(3):
                sums[base + mode, part, pl.ds(8 + start, GROUP), :] = modes[mode][:, part * 128 : (part + 1) * 128]


def join_modes(sums, joint, base):
    for mode in range(6):
        for part in range(3):
            sums[6 + mode, part, pl.ds(0, 8), :] = sums[6 + mode, part, pl.ds(ROWS, 8), :]
            total = sums[mode, part, pl.ds(8, 8, stride=3), :]
            total = total + sums[mode, part, pl.ds(9, 8, stride=3), :]
            total = total + sums[mode, part, pl.ds(10, 8, stride=3), :]
            total = total + sums[6 + mode, part, pl.ds(11, 8, stride=3), :]
            total = total + sums[6 + mode, part, pl.ds(7, 8, stride=3), :]
            joint[pl.ds(base + mode * 8, 8), pl.ds(part * 128, 128)] = total


def reduce_columns(joint):
    node = lax.broadcasted_iota(jnp.int32, (DEPTH, DEPTH // 3), 0)
    block = lax.broadcasted_iota(jnp.int32, (DEPTH, DEPTH // 3), 1)
    groups = (node // 3 == block).astype(jnp.bfloat16)
    rest = joint[...]
    count = rest.shape[0]
    parts = []
    for _ in range(3):
        part = rest.astype(jnp.bfloat16)
        rest = rest - part.astype(jnp.float32)
        parts.append(part)
    three = jnp.dot(jnp.concatenate(parts, axis=0), groups, preferred_element_type=jnp.float32)
    compact = three[:count] + three[count : 2 * count] + three[2 * count :]
    return [compact[row : row + 8] for row in range(0, count, 8)]


def fetch(table, table_held, semaphore):
    copy = pltpu.make_async_copy(table, table_held, semaphore)
    copy.start()
    return copy


def partial_kernel(
    table_in, moved, load, modulus, mask, code, first, second, first_out, second_out, low_out, high_out, middle_out,
    code_out, early_out, from_low, from_high, wide_moved, source, stiff, wide_scaled, sums, joint, low_modes,
    high_modes, table, semaphore,
):
    copy_table = fetch(table_in, table, semaphore)
    take_sides("gy", first, second, from_low, from_high)
    for plane in range(3):
        for comp in range(3):
            halo = joined(from_low, from_high, 3 * (comp * 3 + plane), 3)
            roll_rows(wide_moved, plane * 3 + comp, jnp.concatenate([moved[comp, plane], halo], axis=0))
        out = (low_out.at[slab(STIFF)], stiff, high_out.at[slab(STIFF)])[plane]
        fill_plane(plane, load, modulus, mask, from_low, from_high, source, out, plane)
        out, base = ((low_out, CODE * ROWS), (code_out, 0), (high_out, CODE * ROWS))[plane]
        out[pl.ds(base, OWN), :] = (code[plane] + 1).astype(jnp.float32)
        out[pl.ds(base + OWN, 8), :] = joined(from_low, from_high, 51 + plane, 1)

    copy_table.wait()

    def body(start):
        for plane in range(-1, 4):
            planes = [(other - plane, wide_moved, 3 * other) for other in range(3) if abs(other - plane) < 2]
            product = stencil_rows(table, start, planes, False)
            out = low_out if plane < 2 else high_out
            if plane in (-1, 3):
                for comp in range(3):
                    out[pl.ds(comp * ROWS + start, GROUP), :] = product[comp]
                continue
            factor = stiff[pl.ds(start, GROUP), :] if plane == 1 else out[pl.ds(STIFF * ROWS + start, GROUP), :]
            for comp in range(3):
                loaded = source[plane * 3 + comp, pl.ds(start, GROUP), :]
                residual = loaded - factor * product[comp]
                if plane == 1:
                    middle_out[pl.ds(comp * ROWS + start, GROUP), :] = residual
                else:
                    out[pl.ds((PARTIAL + comp) * ROWS + start, GROUP), :] = residual

    tiles(body)
    for comp in range(3):
        roll_rows(wide_scaled, comp, middle_out[slab(comp), :] / table[13 * 9 + comp * 4])
    for place, (plane, step, out) in enumerate(((3, 1, low_out), (-1, -1, high_out))):

        def middle_part(start, place=place, plane=plane, step=step, out=out):
            product = stencil_rows(table, start, [(step, wide_scaled, 0)], True)
            for comp in range(3):
                early_out[pl.ds((place * 3 + comp) * ROWS + start, GROUP), :] = product[comp]
            stay, leave = ([jnp.zeros((GROUP, DEPTH), jnp.float32) for _ in range(5)] for _ in range(2))
            smoothed = [-smooth_weight * product[comp] for comp in range(3)]
            add_plane(stay, leave, smoothed, out[pl.ds(CODE * ROWS + start, GROUP), :], plane)
            put_modes(stay, leave, start, sums)

        tiles(middle_part)
        join_modes(sums, joint, 48 * place)
    for index, value in enumerate(reduce_columns(joint)):
        (low_modes, high_modes)[index // 6][index % 6] = value

    def copy(even):
        pack_slabs(low_out, low_modes, first_out if even else second_out)
        pack_slabs(high_out, high_modes, second_out if even else first_out)

    on_sides("gx", copy)


def finish_side(table, message, own, residuals, wide_scaled):
    for comp in range(3):
        diagonal = table[13 * 9 + comp * 4]
        for place, (ref, other) in enumerate(((message, own), (own, message))):
            residual = ref[slab(PARTIAL + comp), :] - ref[slab(STIFF), :] * other[slab(comp), :]
            residuals[place * 3 + comp] = residual
            roll_rows(wide_scaled, place * 3 + comp, residual / diagonal)


def side_product(table, start, plane, near, low, wide_scaled):
    sign = 1 if low else -1
    return stencil_rows(table, start, [(sign * (other - plane), wide_scaled, 3 * (other + 1)) for other in near], True)


def add_side(table, start, stay, leave, message, own, early_outer, low, residuals, wide_scaled):
    for plane, ref in ((-1, message), (0, own)):
        product = side_product(table, start, plane, (-1, 0), low, wide_scaled)
        smoothed = []
        for comp in range(3):
            total = product[comp]
            if plane == 0:
                total = total + early_outer[pl.ds(((0 if low else 3) + comp) * ROWS + start, GROUP), :]
            smoothed.append(residuals[(plane + 1) * 3 + comp, pl.ds(start, GROUP), :] - smooth_weight * total)
        code = ref[pl.ds(CODE * ROWS + start, GROUP), :]
        add_plane(stay, leave, smoothed, code, plane if low else 2 - plane)


def first_side_kernel(
    table_in, own_low, own_high, first, middle, early_outer, held_out, product_out, modes_out, message, residuals,
    wide_scaled, scaled_middle, table, semaphore,
):
    copy_table = fetch(table_in, table, semaphore)
    copy_table.wait()
    for comp in range(3):
        roll_rows(scaled_middle, comp, middle[slab(comp), :] / table[13 * 9 + comp * 4])

    def side(low):
        own = own_low if low else own_high
        unpack_slabs(first, message, modes_out)
        finish_side(table, message, own, residuals, wide_scaled)

        def body(start):
            stay, leave = ([jnp.zeros((GROUP, DEPTH), jnp.float32) for _ in range(5)] for _ in range(2))
            add_side(table, start, stay, leave, message, own, early_outer, low, residuals, wide_scaled)
            for index, value in enumerate(stay + leave):
                held_out[pl.ds(index * ROWS + start, GROUP), :] = value
            step = -1 if low else 1
            product = stencil_rows(table, start, [(step, wide_scaled, 3), (0, scaled_middle, 0)], True)
            for comp in range(3):
                product_out[pl.ds(comp * ROWS + start, GROUP), :] = product[comp]

        tiles(body)

    on_sides("gx", side)


def coarse_kernel(
    table_in, own_low, own_high, second, middle, code_middle, early_outer, begun, begun_product, begun_modes, inverse,
    update, message, residuals, wide_scaled, sums, joint, modes, table, semaphore,
):
    copy_table = fetch(table_in, table, semaphore)
    unpack_slabs(second, message, modes)
    copy_table.wait()

    def side(first_low):
        low = not first_low
        own = own_low if low else own_high
        finish_side(table, message, own, residuals, wide_scaled)

        def body(start):
            stay = [begun[pl.ds(index * ROWS + start, GROUP), :] for index in range(5)]
            leave = [begun[pl.ds((5 + index) * ROWS + start, GROUP), :] for index in range(5)]
            add_side(table, start, stay, leave, message, own, early_outer, low, residuals, wide_scaled)
            product = side_product(table, start, 1, (0,), low, wide_scaled)
            smoothed = []
            for comp in range(3):
                rows = pl.ds(comp * ROWS + start, GROUP)
                total = product[comp] + begun_product[rows, :]
                smoothed.append(middle[rows, :] - smooth_weight * total)
            add_plane(stay, leave, smoothed, code_middle[pl.ds(start, GROUP), :], 1)
            put_modes(stay, leave, start, sums)

        tiles(body)

    on_sides("gx", side)
    join_modes(sums, joint, 0)
    coarse = [value + (begun_modes[mode] + modes[mode]) for mode, value in enumerate(reduce_columns(joint))]
    for row in range(6):
        result = inverse[row, 0, 0] * coarse[0]
        for col in range(1, 6):
            result = result + inverse[row, col, 0] * coarse[col]
        update[row, 0] = coarse_weight * result


def exchanged(first, second, axis):
    count = lax.axis_size(axis)
    results = []
    for message, begin in ((first, 1), (second, 0)):
        pairs = [pair for i in range(begin, count - 1, 2) for pair in ((i, i + 1), (i + 1, i))]
        results.append(lax.ppermute(message, axis, pairs))
    return results


def local(
    displacement, applied_load, modulus, free_mask, aggregate_shift, stencil_table, coarse_inverse
):
    f32 = jnp.float32
    table = stencil_table.reshape(243)
    vmem = pl.BlockSpec(memory_space=pltpu.VMEM)
    anywhere = pl.BlockSpec(memory_space=pl.ANY)
    halo_shape = jax.ShapeDtypeStruct((HALO_ROWS, DEPTH), f32)
    first_rows, second_rows = pl.pallas_call(
        pack_kernel,
        in_specs=[pl.BlockSpec(memory_space=pltpu.HBM)] * 5,
        out_specs=(vmem,) * 2,
        out_shape=(halo_shape,) * 2,
        scratch_shapes=[pltpu.VMEM((HALO_ROWS, DEPTH), f32)] * 2
        + [pltpu.VMEM((2, 3, 3, 8, DEPTH), f32)] * 2
        + [pltpu.VMEM((2, 3, 8, DEPTH), f32)]
        + [pltpu.VMEM((2, 3, 8, DEPTH), jnp.int32)] * 2
        + [pltpu.SemaphoreType.DMA((10,))],
        compiler_params=pltpu.CompilerParams(vmem_limit_bytes=56300000),
        name="pack_rows",
    )(displacement, applied_load, modulus, free_mask, aggregate_shift)
    first_rows, second_rows = exchanged(first_rows, second_rows, "gy")

    def rows_of(slabs):
        return jax.ShapeDtypeStruct((slabs * ROWS, DEPTH), f32)

    def held(*shape):
        return pltpu.VMEM(shape + (DEPTH,), f32)

    params = pltpu.CompilerParams(vmem_limit_bytes=VMEM_LIMIT)
    sums = pltpu.VMEM((12, 3, ROWS + 8, 128), f32)
    modes = pltpu.VMEM((6, 8, DEPTH // 3), f32)
    table_held = [pltpu.SMEM((243,), f32), pltpu.SemaphoreType.DMA]
    message = jax.ShapeDtypeStruct((MESSAGE_ROWS, DEPTH), f32)
    first_planes, second_planes, low_planes, high_planes, middle, code_middle, early_outer = pl.pallas_call(
        partial_kernel,
        in_specs=[anywhere] + [vmem] * 7,
        out_specs=(vmem,) * 7,
        out_shape=(message,) * 2 + (rows_of(SLABS),) * 2 + (rows_of(3), rows_of(1), rows_of(6)),
        scratch_shapes=[
            held(HALO_ROWS), held(HALO_ROWS), held(9, 3, ROWS), held(9, ROWS), held(ROWS), held(3, 3, ROWS),
            sums, held(96), modes, modes, *table_held,
        ],
        compiler_params=params,
        name="partial_residual",
    )(table, displacement, applied_load, modulus, free_mask, aggregate_shift, first_rows, second_rows)
    first_planes, second_planes = exchanged(first_planes, second_planes, "gx")

    sides = [held(SLABS * ROWS), held(6, ROWS), held(6, 3, ROWS)]
    begun, begun_product, begun_modes = pl.pallas_call(
        first_side_kernel,
        in_specs=[anywhere] + [vmem] * 5,
        out_specs=(vmem,) * 3,
        out_shape=(rows_of(10), rows_of(3), jax.ShapeDtypeStruct((6, 8, DEPTH // 3), f32)),
        scratch_shapes=sides + [held(3, 3, ROWS), *table_held],
        compiler_params=params,
        name="first_side",
    )(table, low_planes, high_planes, first_planes, middle, early_outer)

    return pl.pallas_call(
        coarse_kernel,
        in_specs=[anywhere] + [vmem] * 10,
        out_specs=vmem,
        out_shape=jax.ShapeDtypeStruct((6, 1, 8, DEPTH // 3), f32),
        scratch_shapes=sides + [sums, held(48), modes, *table_held],
        compiler_params=params,
        name="coarse_update",
    )(
        table, low_planes, high_planes, second_planes, middle, code_middle, early_outer, begun, begun_product,
        begun_modes, coarse_inverse,
    )


def solution(mesh):
    in_specs = (
        P(None, "gx", "gy", None),
        P(None, "gx", "gy", None),
        P("gx", "gy", None),
        P("gx", "gy", None),
        P("gx", "gy", None),
        P(),
        P(None, None, "gx", "gy", None),
    )
    out_specs = P(None, "gx", "gy", None)
    return jax.shard_map(local, mesh=mesh, in_specs=in_specs, out_specs=out_specs, check_vma=False)
```

```python
import jax
import jax.numpy as jnp
from jax import lax
from jax.experimental import pallas as pl
from jax.experimental.pallas import tpu as pltpu
from jax.sharding import PartitionSpec as P

smooth_weight = 0.6
coarse_weight = 0.7

ROWS = 32
OWN = 24
DEPTH = 384
SLABS = 8
PARTIAL = 3
STIFF = 6
CODE = 7
BESIDE = SLABS * OWN
MODES = BESIDE + SLABS * 4
MESSAGE_ROWS = MODES + 16
GROUP = 32
HALO_ROWS = 56
VMEM_LIMIT = 48 * 1024 * 1024


def slab(index):
    return pl.ds(index * ROWS, ROWS)


def pack_kernel(
    moved_all, load_all, modulus_all, mask_all, code_all, first_out, second_out, moved, load, modulus,
    mask, code, semaphores,
):
    copies = []
    for index, (whole, held) in enumerate(
        ((moved_all, moved), (load_all, load), (modulus_all, modulus), (mask_all, mask), (code_all, code))
    ):
        for side, begin in enumerate((0, OWN - 8)):
            rows = pl.ds(begin, 8)
            source = whole.at[:, :, rows, :] if index < 2 else whole.at[:, rows, :]
            copies.append(pltpu.make_async_copy(source, held.at[side], semaphores.at[2 * index + side]))
    for copy in copies:
        copy.start()
    for copy in copies:
        copy.wait()

    def fill(out, side, first_moved, first_load, first_code):
        for plane in range(3):
            freedom = mask[side, plane, pl.ds(first_load, 2), :].astype(jnp.float32)
            for comp in range(3):
                unit = comp * 3 + plane
                out[pl.ds(3 * unit, 3), :] = moved[side, comp, plane, pl.ds(first_moved, 3), :]
                out[pl.ds(27 + 2 * unit, 2), :] = freedom * load[side, comp, plane, pl.ds(first_load, 2), :]
            out[pl.ds(45 + 2 * plane, 2), :] = freedom * modulus[side, plane, pl.ds(first_load, 2), :]
            out[pl.ds(51 + plane, 1), :] = (code[side, plane, pl.ds(first_code, 1), :] + 1).astype(jnp.float32)
        out[pl.ds(54, 2), :] = jnp.zeros((2, DEPTH), jnp.float32)

    def both(even):
        fill(first_out if even else second_out, 0, 0, 0, 0)
        fill(second_out if even else first_out, 1, 5, 6, 7)

    on_sides("gy", both)


def on_sides(axis, copy):
    even = lax.axis_index(axis) % 2 == 0
    pl.when(even)(lambda: copy(True))
    pl.when(jnp.logical_not(even))(lambda: copy(False))


def take_sides(axis, first, second, low_out, high_out):
    def copy(even):
        low_out[...] = first[...] if even else second[...]
        high_out[...] = second[...] if even else first[...]

    on_sides(axis, copy)


def pack_slabs(slabs, modes, out):
    row = lax.broadcasted_iota(jnp.int32, (8, DEPTH), 0)
    near = (row < 2) | (row > 5)
    for index in range(SLABS):
        out[pl.ds(index * OWN, OWN), :] = slabs[pl.ds(index * ROWS, OWN), :]
    for index in range(0, SLABS, 2):
        one = slabs[pl.ds(index * ROWS + OWN, 8), :]
        other = pltpu.roll(slabs[pl.ds((index + 1) * ROWS + OWN, 8), :], 4, 0)
        out[pl.ds(BESIDE + index * 4, 8), :] = jnp.where(near, one, other)
    for mode in range(6):
        out[pl.ds(MODES + mode // 3 * 8, 8), pl.ds(mode % 3 * 128, 128)] = modes[mode]


def unpack_slabs(message, slabs, modes):
    for index in range(SLABS):
        slabs[pl.ds(index * ROWS, OWN), :] = message[pl.ds(index * OWN, OWN), :]
    for index in range(0, SLABS, 2):
        both = message[pl.ds(BESIDE + index * 4, 8), :]
        slabs[pl.ds(index * ROWS + OWN, 8), :] = both
        slabs[pl.ds((index + 1) * ROWS + OWN, 8), :] = pltpu.roll(both, 4, 0)
    for mode in range(6):
        modes[mode] = message[pl.ds(MODES + mode // 3 * 8, 8), pl.ds(mode % 3 * 128, 128)]


def roll_rows(ref, index, value):
    ref[index, 0] = pltpu.roll(value, 1, 0)
    ref[index, 1] = value
    ref[index, 2] = pltpu.roll(value, ROWS - 1, 0)


def stencil_rows(table, start, planes, flipped):
    column = lax.broadcasted_iota(jnp.int32, (GROUP, DEPTH), 1)
    outputs = []
    for row in range(3):
        totals = [None] * 3
        for step_x, ref, base in planes:
            for step_y in (-1, 0, 1):
                for col in range(3):
                    value = ref[base + col, step_y + 1, pl.ds(start, GROUP), :]
                    for step_z in (-1, 0, 1):
                        offset = 9 * (step_x + 1) + 3 * (step_y + 1) + step_z + 1
                        entry = (26 - offset) * 9 + col * 3 + row if flipped else offset * 9 + row * 3 + col
                        term = table[entry] * value
                        old = totals[step_z + 1]
                        totals[step_z + 1] = term if old is None else old + term
        below, same, above = totals
        below = jnp.where(column == 0, 0.0, pltpu.roll(below, 1, 1))
        above = jnp.where(column == DEPTH - 1, 0.0, pltpu.roll(above, DEPTH - 1, 1))
        outputs.append(same + below + above)
    return outputs


def joined(from_low, from_high, first, count):
    rows = jnp.zeros((8, DEPTH), jnp.float32)
    place = lax.broadcasted_iota(jnp.int32, (8, DEPTH), 0)
    for step in range(count):
        rows = jnp.where(place == step, from_high[pl.ds(first + step, 1), :], rows)
        rows = jnp.where(place == 8 - count + step, from_low[pl.ds(first + step, 1), :], rows)
    return rows


def tiles(body):
    for start in range(0, ROWS, GROUP):
        body(start)


def fill_plane(plane, load, modulus, mask, from_low, from_high, source, stiff, index):
    halo = pl.ds(OWN, 8)
    freedom = mask[plane].astype(jnp.float32)
    for comp in range(3):
        source[index * 3 + comp, pl.ds(0, OWN), :] = freedom * load[comp, plane]
        source[index * 3 + comp, halo, :] = joined(from_low, from_high, 27 + 2 * (comp * 3 + plane), 2)
    stiff[pl.ds(0, OWN), :] = freedom * modulus[plane]
    stiff[halo, :] = joined(from_low, from_high, 45 + 2 * plane, 2)


def add_plane(stay, leave, smoothed, code, plane):
    middle = 3.0 * (1 if plane == -1 else -1 if plane == 3 else 0) + 5.0
    stays = code == middle
    leaves = (code == middle - 1.0) | (code == middle + 1.0)
    arm = float(plane - 1)
    for held, chosen in ((stay, stays), (leave, leaves)):
        for comp in range(3):
            picked = jnp.where(chosen, smoothed[comp], 0.0)
            held[comp] = held[comp] + picked
            if comp > 0 and arm != 0.0:
                held[2 + comp] = held[2 + comp] + arm * picked


def put_modes(stay, leave, start, sums):
    shape = (GROUP, DEPTH)
    row = lax.broadcasted_iota(jnp.int32, shape, 0) + start
    row = jnp.where(row == ROWS - 1, 2, row) % 3
    lever_z = (lax.broadcasted_iota(jnp.int32, shape, 1) % 3 - 1).astype(jnp.float32)
    lever_stay = (row - 1).astype(jnp.float32)
    lever_leave = jnp.where(row == 0, 2.0, jnp.where(row == 2, -2.0, 0.0))
    for held, lever_y, base in ((stay, lever_stay, 0), (leave, lever_leave, 6)):
        push_x, push_y, push_z, armed_y, armed_z = held
        modes = (
            push_x, push_y, push_z,
            lever_y * push_z - lever_z * push_y,
            lever_z * push_x - armed_z,
            armed_y - lever_y * push_x,
        )
        for mode in range(6):
            for part in range(3):
                sums[base + mode, part, pl.ds(8 + start, GROUP), :] = modes[mode][:, part * 128 : (part + 1) * 128]


def join_modes(sums, joint, base):
    for mode in range(6):
        for part in range(3):
            sums[6 + mode, part, pl.ds(0, 8), :] = sums[6 + mode, part, pl.ds(ROWS, 8), :]
            total = sums[mode, part, pl.ds(8, 8, stride=3), :]
            total = total + sums[mode, part, pl.ds(9, 8, stride=3), :]
            total = total + sums[mode, part, pl.ds(10, 8, stride=3), :]
            total = total + sums[6 + mode, part, pl.ds(11, 8, stride=3), :]
            total = total + sums[6 + mode, part, pl.ds(7, 8, stride=3), :]
            joint[pl.ds(base + mode * 8, 8), pl.ds(part * 128, 128)] = total


def reduce_columns(joint):
    node = lax.broadcasted_iota(jnp.int32, (DEPTH, DEPTH // 3), 0)
    block = lax.broadcasted_iota(jnp.int32, (DEPTH, DEPTH // 3), 1)
    groups = (node // 3 == block).astype(jnp.bfloat16)
    rest = joint[...]
    count = rest.shape[0]
    parts = []
    for _ in range(3):
        part = rest.astype(jnp.bfloat16)
        rest = rest - part.astype(jnp.float32)
        parts.append(part)
    three = jnp.dot(jnp.concatenate(parts, axis=0), groups, preferred_element_type=jnp.float32)
    compact = three[:count] + three[count : 2 * count] + three[2 * count :]
    return [compact[row : row + 8] for row in range(0, count, 8)]


def fetch(table, table_held, semaphore):
    copy = pltpu.make_async_copy(table, table_held, semaphore)
    copy.start()
    return copy


def partial_kernel(
    table_in, moved, load, modulus, mask, code, first, second, first_out, second_out, low_out, high_out, middle_out,
    code_out, early_out, from_low, from_high, wide_moved, source, stiff, wide_scaled, sums, joint, low_modes,
    high_modes, table, semaphore,
):
    copy_table = fetch(table_in, table, semaphore)
    take_sides("gy", first, second, from_low, from_high)
    for plane in range(3):
        for comp in range(3):
            halo = joined(from_low, from_high, 3 * (comp * 3 + plane), 3)
            roll_rows(wide_moved, plane * 3 + comp, jnp.concatenate([moved[comp, plane], halo], axis=0))
        out = (low_out.at[slab(STIFF)], stiff, high_out.at[slab(STIFF)])[plane]
        fill_plane(plane, load, modulus, mask, from_low, from_high, source, out, plane)
        out, base = ((low_out, CODE * ROWS), (code_out, 0), (high_out, CODE * ROWS))[plane]
        out[pl.ds(base, OWN), :] = (code[plane] + 1).astype(jnp.float32)
        out[pl.ds(base + OWN, 8), :] = joined(from_low, from_high, 51 + plane, 1)

    copy_table.wait()

    def body(start):
        for plane in range(-1, 4):
            planes = [(other - plane, wide_moved, 3 * other) for other in range(3) if abs(other - plane) < 2]
            product = stencil_rows(table, start, planes, False)
            out = low_out if plane < 2 else high_out
            if plane in (-1, 3):
                for comp in range(3):
                    out[pl.ds(comp * ROWS + start, GROUP), :] = product[comp]
                continue
            factor = stiff[pl.ds(start, GROUP), :] if plane == 1 else out[pl.ds(STIFF * ROWS + start, GROUP), :]
            for comp in range(3):
                loaded = source[plane * 3 + comp, pl.ds(start, GROUP), :]
                residual = loaded - factor * product[comp]
                if plane == 1:
                    middle_out[pl.ds(comp * ROWS + start, GROUP), :] = residual
                else:
                    out[pl.ds((PARTIAL + comp) * ROWS + start, GROUP), :] = residual

    tiles(body)
    for comp in range(3):
        roll_rows(wide_scaled, comp, middle_out[slab(comp), :] / table[13 * 9 + comp * 4])
    for place, (plane, step, out) in enumerate(((3, 1, low_out), (-1, -1, high_out))):

        def middle_part(start, place=place, plane=plane, step=step, out=out):
            product = stencil_rows(table, start, [(step, wide_scaled, 0)], True)
            for comp in range(3):
                early_out[pl.ds((place * 3 + comp) * ROWS + start, GROUP), :] = product[comp]
            stay, leave = ([jnp.zeros((GROUP, DEPTH), jnp.float32) for _ in range(5)] for _ in range(2))
            smoothed = [-smooth_weight * product[comp] for comp in range(3)]
            add_plane(stay, leave, smoothed, out[pl.ds(CODE * ROWS + start, GROUP), :], plane)
            put_modes(stay, leave, start, sums)

        tiles(middle_part)
        join_modes(sums, joint, 48 * place)
    for index, value in enumerate(reduce_columns(joint)):
        (low_modes, high_modes)[index // 6][index % 6] = value

    def copy(even):
        pack_slabs(low_out, low_modes, first_out if even else second_out)
        pack_slabs(high_out, high_modes, second_out if even else first_out)

    on_sides("gx", copy)


def finish_side(table, message, own, residuals, wide_scaled):
    for comp in range(3):
        diagonal = table[13 * 9 + comp * 4]
        for place, (ref, other) in enumerate(((message, own), (own, message))):
            residual = ref[slab(PARTIAL + comp), :] - ref[slab(STIFF), :] * other[slab(comp), :]
            residuals[place * 3 + comp] = residual
            roll_rows(wide_scaled, place * 3 + comp, residual / diagonal)


def side_product(table, start, plane, near, low, wide_scaled):
    sign = 1 if low else -1
    return stencil_rows(table, start, [(sign * (other - plane), wide_scaled, 3 * (other + 1)) for other in near], True)


def add_side(table, start, stay, leave, message, own, early_outer, low, residuals, wide_scaled):
    for plane, ref in ((-1, message), (0, own)):
        product = side_product(table, start, plane, (-1, 0), low, wide_scaled)
        smoothed = []
        for comp in range(3):
            total = product[comp]
            if plane == 0:
                total = total + early_outer[pl.ds(((0 if low else 3) + comp) * ROWS + start, GROUP), :]
            smoothed.append(residuals[(plane + 1) * 3 + comp, pl.ds(start, GROUP), :] - smooth_weight * total)
        code = ref[pl.ds(CODE * ROWS + start, GROUP), :]
        add_plane(stay, leave, smoothed, code, plane if low else 2 - plane)


def first_side_kernel(
    table_in, own_low, own_high, first, middle, early_outer, held_out, product_out, modes_out, message, residuals,
    wide_scaled, scaled_middle, table, semaphore,
):
    copy_table = fetch(table_in, table, semaphore)
    copy_table.wait()
    for comp in range(3):
        roll_rows(scaled_middle, comp, middle[slab(comp), :] / table[13 * 9 + comp * 4])

    def side(low):
        own = own_low if low else own_high
        unpack_slabs(first, message, modes_out)
        finish_side(table, message, own, residuals, wide_scaled)

        def body(start):
            stay, leave = ([jnp.zeros((GROUP, DEPTH), jnp.float32) for _ in range(5)] for _ in range(2))
            add_side(table, start, stay, leave, message, own, early_outer, low, residuals, wide_scaled)
            for index, value in enumerate(stay + leave):
                held_out[pl.ds(index * ROWS + start, GROUP), :] = value
            step = -1 if low else 1
            product = stencil_rows(table, start, [(step, wide_scaled, 3), (0, scaled_middle, 0)], True)
            for comp in range(3):
                product_out[pl.ds(comp * ROWS + start, GROUP), :] = product[comp]

        tiles(body)

    on_sides("gx", side)


def coarse_kernel(
    table_in, own_low, own_high, second, middle, code_middle, early_outer, begun, begun_product, begun_modes, inverse,
    update, message, residuals, wide_scaled, sums, joint, modes, table, semaphore,
):
    copy_table = fetch(table_in, table, semaphore)
    unpack_slabs(second, message, modes)
    copy_table.wait()

    def side(first_low):
        low = not first_low
        own = own_low if low else own_high
        finish_side(table, message, own, residuals, wide_scaled)

        def body(start):
            stay = [begun[pl.ds(index * ROWS + start, GROUP), :] for index in range(5)]
            leave = [begun[pl.ds((5 + index) * ROWS + start, GROUP), :] for index in range(5)]
            add_side(table, start, stay, leave, message, own, early_outer, low, residuals, wide_scaled)
            product = side_product(table, start, 1, (0,), low, wide_scaled)
            smoothed = []
            for comp in range(3):
                rows = pl.ds(comp * ROWS + start, GROUP)
                total = product[comp] + begun_product[rows, :]
                smoothed.append(middle[rows, :] - smooth_weight * total)
            add_plane(stay, leave, smoothed, code_middle[pl.ds(start, GROUP), :], 1)
            put_modes(stay, leave, start, sums)

        tiles(body)

    on_sides("gx", side)
    join_modes(sums, joint, 0)
    coarse = [value + (begun_modes[mode] + modes[mode]) for mode, value in enumerate(reduce_columns(joint))]
    for row in range(6):
        result = inverse[row, 0, 0] * coarse[0]
        for col in range(1, 6):
            result = result + inverse[row, col, 0] * coarse[col]
        update[row, 0] = coarse_weight * result


def exchanged(first, second, axis):
    count = lax.axis_size(axis)
    results = []
    for message, begin in ((first, 1), (second, 0)):
        pairs = [pair for i in range(begin, count - 1, 2) for pair in ((i, i + 1), (i + 1, i))]
        results.append(lax.ppermute(message, axis, pairs))
    return results


def local(
    displacement, applied_load, modulus, free_mask, aggregate_shift, stencil_table, coarse_inverse
):
    f32 = jnp.float32
    table = stencil_table.reshape(243)
    vmem = pl.BlockSpec(memory_space=pltpu.VMEM)
    anywhere = pl.BlockSpec(memory_space=pl.ANY)
    halo_shape = jax.ShapeDtypeStruct((HALO_ROWS, DEPTH), f32)
    first_rows, second_rows = pl.pallas_call(
        pack_kernel,
        in_specs=[pl.BlockSpec(memory_space=pltpu.HBM)] * 5,
        out_specs=(vmem,) * 2,
        out_shape=(halo_shape,) * 2,
        scratch_shapes=[pltpu.VMEM((2, 3, 3, 8, DEPTH), f32)] * 2
        + [pltpu.VMEM((2, 3, 8, DEPTH), f32)]
        + [pltpu.VMEM((2, 3, 8, DEPTH), jnp.int32)] * 2
        + [pltpu.SemaphoreType.DMA((10,))],
        compiler_params=pltpu.CompilerParams(vmem_limit_bytes=56300000),
        name="pack_rows",
    )(displacement, applied_load, modulus, free_mask, aggregate_shift)
    first_rows, second_rows = exchanged(first_rows, second_rows, "gy")

    def rows_of(slabs):
        return jax.ShapeDtypeStruct((slabs * ROWS, DEPTH), f32)

    def held(*shape):
        return pltpu.VMEM(shape + (DEPTH,), f32)

    params = pltpu.CompilerParams(vmem_limit_bytes=VMEM_LIMIT)
    sums = pltpu.VMEM((12, 3, ROWS + 8, 128), f32)
    modes = pltpu.VMEM((6, 8, DEPTH // 3), f32)
    table_held = [pltpu.SMEM((243,), f32), pltpu.SemaphoreType.DMA]
    message = jax.ShapeDtypeStruct((MESSAGE_ROWS, DEPTH), f32)
    first_planes, second_planes, low_planes, high_planes, middle, code_middle, early_outer = pl.pallas_call(
        partial_kernel,
        in_specs=[anywhere] + [vmem] * 7,
        out_specs=(vmem,) * 7,
        out_shape=(message,) * 2 + (rows_of(SLABS),) * 2 + (rows_of(3), rows_of(1), rows_of(6)),
        scratch_shapes=[
            held(HALO_ROWS), held(HALO_ROWS), held(9, 3, ROWS), held(9, ROWS), held(ROWS), held(3, 3, ROWS),
            sums, held(96), modes, modes, *table_held,
        ],
        compiler_params=params,
        name="partial_residual",
    )(table, displacement, applied_load, modulus, free_mask, aggregate_shift, first_rows, second_rows)
    first_planes, second_planes = exchanged(first_planes, second_planes, "gx")

    sides = [held(SLABS * ROWS), held(6, ROWS), held(6, 3, ROWS)]
    begun, begun_product, begun_modes = pl.pallas_call(
        first_side_kernel,
        in_specs=[anywhere] + [vmem] * 5,
        out_specs=(vmem,) * 3,
        out_shape=(rows_of(10), rows_of(3), jax.ShapeDtypeStruct((6, 8, DEPTH // 3), f32)),
        scratch_shapes=sides + [held(3, 3, ROWS), *table_held],
        compiler_params=params,
        name="first_side",
    )(table, low_planes, high_planes, first_planes, middle, early_outer)

    return pl.pallas_call(
        coarse_kernel,
        in_specs=[anywhere] + [vmem] * 10,
        out_specs=vmem,
        out_shape=jax.ShapeDtypeStruct((6, 1, 8, DEPTH // 3), f32),
        scratch_shapes=sides + [sums, held(48), modes, *table_held],
        compiler_params=params,
        name="coarse_update",
    )(
        table, low_planes, high_planes, second_planes, middle, code_middle, early_outer, begun, begun_product,
        begun_modes, coarse_inverse,
    )


def solution(mesh):
    in_specs = (
        P(None, "gx", "gy", None),
        P(None, "gx", "gy", None),
        P("gx", "gy", None),
        P("gx", "gy", None),
        P("gx", "gy", None),
        P(),
        P(None, None, "gx", "gy", None),
    )
    out_specs = P(None, "gx", "gy", None)
    return jax.shard_map(local, mesh=mesh, in_specs=in_specs, out_specs=out_specs, check_vma=False)
```
